128 devices in a mesh: seq: 32 (over x, z_lo, y), grp: 4 (over z_hi, core).
Axes of the slice: x: 4, y: 4, z: 4 (z_hi: 2, z_lo: 2; z = z_hi * 2 + z_lo), core: 2. Of those that a mesh axis runs over, the one named last changes fastest.
Arguments:
- query: bfloat16 [196608, 512], P('seq', 'grp'), may hold values from -6 to 6
- pos_emb: bfloat16 [196608, 512], P('seq', 'grp'), may hold values from -5 to 5
- pos_ids: int32 [196608], P('seq'), may hold values from 0 to 1048575
- lengths: int32 [32, 32], P('seq'), may hold values from 1 to 192, 2048 in all within a row
- negatives: bfloat16 [2048, 512], P(('seq', 'grp')), may hold values from -100 to 100
- neg_ids: int32 [2048], P(('seq', 'grp')), may hold values from 0 to 1048575
Outputs:
- grad_query: bfloat16 [196608, 512], P('seq', 'grp')
- grad_items: float32 [2048, 512], P(('seq', 'grp'))
The draws below stay inside these ranges and needn't reach their ends.
Inputs may be any that keep to these rules, and one draw needn't show every extreme that they name: Each row of 32 lengths sums to 2048, and every row holds one length of exactly 192.
All inputs are finite; a program needn't handle non-finite values.
Results may differ from the reference program's by a relative error of at most 0.0037.
Values may be sent and summed in bfloat16 or wider, within the bound.
No kernel may reach another device: no remote copies, remote signals or barrier semaphores. Data moves between devices by JAX's collectives and lax.ppermute only.
A program may use at most 64 MiB of HBM per device.

```python
import math
import jax
import jax.numpy as jnp
import numpy as np
from jax import lax

D = 512
CATALOG = 1048576
POPULAR = 16
MAXLEN = 192
HIST_G = 32
TOTAL_G = 2048
SLOT_G = 6144
SLOTS = 196608
NEG = 2048
N_SEQ = 32


def popular_table(key):
    table_key = jax.random.fold_in(key, 5)
    table = jax.random.randint(table_key, (POPULAR,), 0, CATALOG, dtype=jnp.int32)
    table = table.at[0].set(0)
    return table.at[1].set(CATALOG - 1)


def mixed_ids(table, key, count, popular_of_four):
    key_pick, key_free, key_use = jax.random.split(key, 3)
    pick = jax.random.randint(key_pick, (count,), 0, POPULAR, dtype=jnp.int32)
    free_ids = jax.random.randint(key_free, (count,), 0, CATALOG, dtype=jnp.int32)
    use_table = jax.random.randint(key_use, (count,), 0, 4, dtype=jnp.int32) < popular_of_four
    return jnp.where(use_table, jnp.take(table, pick), free_ids).astype(jnp.int32)


def draw_pos_ids(key, part):
    table = popular_table(key)
    key = jax.random.fold_in(key, 31)
    return mixed_ids(table, key, SLOTS, 3)


def draw_neg_ids(key, part):
    table = popular_table(key)
    key = jax.random.fold_in(key, 37)
    return mixed_ids(table, key, NEG, 2)


def draw_query(key, part):
    key = jax.random.fold_in(key, 11)
    key_base = jax.random.fold_in(key, 0)
    values = 0.15 * jax.random.normal(key_base, (SLOTS, D), jnp.float32)
    return jnp.clip(values, -6.0, 6.0).astype(jnp.bfloat16)


def draw_negatives(key, part):
    key = jax.random.fold_in(key, 23)
    key_base = jax.random.fold_in(key, 0)
    values = jnp.clip(0.88 * jax.random.normal(key_base, (NEG, D), jnp.float32), -5.0, 5.0)
    return values.astype(jnp.bfloat16)


def shard_levels(rng, dims, cuts, low, top_value):
    def one(dim, parts):
        steps = jax.random.uniform(jax.random.fold_in(jax.random.fold_in(rng, 6), dim), (parts,), jnp.float32, low / len(cuts), top_value / len(cuts))
        return jnp.repeat(jnp.exp(steps), dims[dim] // parts).reshape((-1,) + (1,) * (len(dims) - dim - 1))

    loudness = one(*cuts[0])
    for cut in cuts[1:]:
        loudness = loudness * one(*cut)
    return loudness


def split_up(amount, total, bound, lean):
    loads = [(1 << 20) // math.isqrt(standing ** lean) + 1 for standing in range(2, amount + 1)]
    surplus, holding = total - bound - (amount - 1), [1] * (amount - 1)
    while surplus > 0:
        free = [i for i in range(amount - 1) if holding[i] < bound]
        pool, left = sum([loads[i] for i in free]), surplus
        for i in free:
            more = min(bound - holding[i], max(1, left * loads[i] // pool), surplus)
            holding[i] = holding[i] + more
            surplus = surplus - more
    return np.array([bound] + holding)


def ragged(stream_key, count, total, most, slope):
    if count == 2:
        one = jax.random.randint(stream_key, (), max(1, total - most), min(most, total - 1) + 1)
        return jnp.stack([one, total - one])
    sizes = jnp.asarray(split_up(count, total, most, slope), jnp.int32)
    pairs = (count - 1) // 2
    donor, taker = sizes[1:1 + 2 * pairs:2], sizes[2:2 + 2 * pairs:2]
    margin = jnp.minimum(donor - 1, most - taker)
    passed = jax.random.randint(jax.random.fold_in(stream_key, 1), (pairs,), 0, 1 << 20) % (margin + 1)
    sizes = sizes.at[1:1 + 2 * pairs:2].set(donor - passed).at[2:2 + 2 * pairs:2].set(taker + passed)
    return sizes[jax.random.permutation(jax.random.fold_in(stream_key, 2), count)]


def centred(key, shape, spread, reach, pieces=(), kind=jnp.bfloat16):
    level = shard_levels(key, shape, pieces, -0.22, 0.18) if pieces else 1.0
    entries = jax.random.normal(key, shape, jnp.float32) * spread * level
    return jnp.minimum(jnp.maximum(entries, -reach), reach).astype(kind)


def setup_inputs(seed: int = 0) -> dict:
    key_list = jax.random.split(jax.random.key(seed), 7)
    return {
        "query": draw_query(jax.random.fold_in(key_list[6], 71), 0),
        "pos_emb": centred(key_list[1], (SLOTS, D), 0.88, 5.0, ((0, 32), (1, 4))),
        "pos_ids": draw_pos_ids(jax.random.fold_in(key_list[6], 71), 0),
        "lengths": jax.vmap(lambda own: ragged(own, HIST_G, TOTAL_G, MAXLEN, 2))(jax.random.split(key_list[3], N_SEQ)).reshape((N_SEQ, HIST_G)).astype(jnp.int32),
        "negatives": draw_negatives(jax.random.fold_in(key_list[6], 71), 0),
        "neg_ids": draw_neg_ids(jax.random.fold_in(key_list[6], 71), 0),
    }


def packed_slots(length_row):
    hist_ends = jnp.cumsum(length_row).astype(jnp.int32)
    hist_starts = (hist_ends - length_row).astype(jnp.int32)
    packed = jnp.arange(TOTAL_G, dtype=jnp.int32)
    history = jnp.sum((packed[:, None] >= hist_ends[None, :]).astype(jnp.int32), axis=1)
    first_row = jnp.take(hist_starts, history)
    return (history * MAXLEN + packed - first_row).astype(jnp.int32)


def group_grads(inputs, negatives, neg_ids):
    query_g, pos_g, ids_g, length_row = inputs
    slot_list = packed_slots(length_row)
    rows_q = jnp.take(query_g, slot_list, axis=0)
    rows_p = jnp.take(pos_g, slot_list, axis=0)
    rows_id = jnp.take(ids_g, slot_list)
    scores = jnp.dot(rows_q, negatives.T, preferred_element_type=jnp.float32)
    positive = jnp.sum(rows_q.astype(jnp.float32) * rows_p.astype(jnp.float32), axis=1)
    collide = rows_id[:, None] == neg_ids[None, :]
    masked = jnp.where(collide, -jnp.inf, scores)
    row_top = jnp.maximum(jnp.max(masked, axis=1), positive)
    denominator = jnp.exp(positive - row_top) + jnp.sum(jnp.exp(masked - row_top[:, None]), axis=1)
    log_total = row_top + jnp.log(denominator)
    weights = jnp.exp(masked - log_total[:, None]).astype(jnp.bfloat16)
    own_term = jnp.exp(positive - log_total) - 1.0
    grad_rows = jnp.dot(weights, negatives, preferred_element_type=jnp.float32) + own_term[:, None] * rows_p.astype(jnp.float32)
    grad_q = jnp.zeros(query_g.shape, jnp.bfloat16).at[slot_list].set(grad_rows.astype(jnp.bfloat16))
    grad_n = jnp.dot(weights.T, rows_q, preferred_element_type=jnp.float32)
    return grad_q, grad_n


def reference(query, pos_emb, pos_ids, lengths, negatives, neg_ids):
    shaped = (query.reshape(N_SEQ, SLOT_G, D), pos_emb.reshape(N_SEQ, SLOT_G, D), pos_ids.reshape(N_SEQ, SLOT_G), lengths)

    def one_group(carried, inputs):
        grad_q, grad_n = group_grads(inputs, negatives, neg_ids)
        return carried + grad_n, grad_q

    start_sum = jnp.zeros((NEG, D), jnp.float32)
    grad_items, grad_query = lax.scan(one_group, start_sum, shaped)
    return grad_query.reshape(SLOTS, D), grad_items
```

```python
from functools import partial

import jax
import jax.numpy as jnp
from jax import lax
from jax.experimental import pallas as pl
from jax.experimental.pallas import tpu as pltpu
from jax.sharding import PartitionSpec as P

MAXLEN = 192
LANES = 128
CHUNK = 64
FLOOR = -1e30
MASKED = -3e38
F32 = jnp.float32
BF16 = jnp.bfloat16
VMEM_BYTES = 56 * 1024 * 1024


def params():
    return pltpu.CompilerParams(vmem_limit_bytes=VMEM_BYTES)


def whole():
    return pl.BlockSpec(memory_space=pltpu.VMEM)


def small():
    return pl.BlockSpec(memory_space=pltpu.SMEM)


def dot(a, b, da, db):
    return lax.dot_general(a, b, (((da,), (db,)), ((), ())), preferred_element_type=F32)


def copy_rows(len_ref, src_ref, packed):
    start = jnp.int32(0)
    for h in range(len_ref.shape[1]):
        size = len_ref[0, h]
        for c in range(0, MAXLEN, CHUNK):

            @pl.when(size > c)
            def _():
                packed[pl.ds(start + c, CHUNK), :] = src_ref[h * MAXLEN + c : h * MAXLEN + c + CHUNK, :].astype(F32)

        start = start + size


def pack_query(len_ref, q_ref, qp_ref, packed):
    copy_rows(len_ref, q_ref, packed)
    qp_ref[...] = packed[: qp_ref.shape[0], :].astype(BF16)


def pack_positive(len_ref, p_ref, id_ref, qp_ref, pp_ref, part_ref, idp_ref, packed, ids):
    rows = pp_ref.shape[0]
    copy_rows(len_ref, p_ref, packed)
    held = packed[:rows, :]
    pp_ref[...] = held.astype(BF16)
    product = held * qp_ref[...].astype(F32)
    high = product.astype(BF16)
    low = (product - high.astype(F32)).astype(BF16)
    ones = jnp.ones((16, LANES), BF16)
    part_ref[...] = (dot(ones, high, 1, 1) + dot(ones, low, 1, 1))[:1, :]
    lane = lax.broadcasted_iota(jnp.int32, (1, LANES), 1)
    start = jnp.int32(0)
    for h in range(len_ref.shape[1]):
        row, off = divmod(h * MAXLEN, LANES)
        at = start + (LANES - off)
        target = at // LANES
        shift = at - target * LANES
        first = pltpu.roll(id_ref[row : row + 1, :], shift, 1)
        second = pltpu.roll(id_ref[row + 1 : row + 2, :], shift, 1)
        kept0 = ids[pl.ds(target, 1), :]
        kept1 = ids[pl.ds(target + 1, 1), :]
        ids[pl.ds(target, 1), :] = jnp.where(lane >= shift + off, first, kept0)
        ids[pl.ds(target + 1, 1), :] = jnp.where(
            lane + LANES >= shift + off, jnp.where(lane >= shift, second, first), kept1
        )
        ids[pl.ds(target + 2, 1), :] = second
        start = start + len_ref[0, h]
    for k in range(rows // LANES):
        idp_ref[:, k * LANES : (k + 1) * LANES] = ids[k + 1 : k + 2, :].astype(F32)


def block_of(order, step):
    return pl.ds(pl.multiple_of((order ^ step) * LANES, LANES), LANES)


def scores_kernel(neg_ref, q0_ref, q1_ref, q2_ref, q3_ref, idp_ref, part_ref, qfull_ref, e_ref, stat_ref, negid):
    member = lax.axis_index("grp")
    width = 4 * LANES

    @pl.when(pl.program_id(0) == 0)
    def _():
        lane = lax.broadcasted_iota(jnp.int32, (1, LANES), 1)
        place = jnp.where(lane == 0, 65536.0, jnp.where(lane == 1, 256.0, jnp.where(lane == 2, 1.0, 0.0)))
        value = jnp.sum(neg_ref[:, width : width + LANES].astype(F32) * place, axis=1, keepdims=True)
        negid[...] = jnp.broadcast_to(value, negid.shape)

    for k, ref in enumerate((q0_ref, q1_ref, q2_ref, q3_ref)):
        qfull_ref[:, block_of(member, k)] = ref[...]
    scores = dot(neg_ref[:, :width], qfull_ref[...], 1, 1)
    for k in range(scores.shape[1] // LANES):
        at = slice(k * LANES, (k + 1) * LANES)
        part = jnp.where(negid[...] == idp_ref[:, at], MASKED, scores[:, at])
        top = jnp.maximum(jnp.max(part, axis=0, keepdims=True), FLOOR)
        e = jnp.exp(part - top)
        e_ref[:, at] = e
        stat_ref[0:1, at] = top
        stat_ref[1:2, at] = jnp.sum(e, axis=0, keepdims=True)
        stat_ref[2:3, at] = part_ref[:, at]
        stat_ref[3:4, at] = part_ref[:, at]


def rows_kernel(neg_ref, e_ref, keep_ref, send_ref, turned):
    member = lax.axis_index("grp")
    half = 2 * LANES

    @pl.when(pl.program_id(0) == 0)
    def _():
        for k, step in enumerate((0, 2, 1, 3)):
            turned[k * LANES : (k + 1) * LANES, :] = neg_ref[:, block_of(member, step)].T

    out = dot(turned[...], e_ref[...].astype(BF16), 1, 0)
    keep_ref[...] = out[:half, :]
    send_ref[...] = out[half:, :].astype(BF16)


def totals(refs):
    positive = refs[0][2:3, :] + refs[1][2:3, :] + refs[2][2:3, :] + refs[3][2:3, :]
    top = positive
    for ref in refs:
        top = jnp.maximum(top, ref[0:1, :])
    total = jnp.exp(positive - top)
    for ref in refs:
        total = total + ref[1:2, :] * jnp.exp(ref[0:1, :] - top)
    return positive, top + jnp.log(total)


def combine_kernel(s0, s1, s2, s3, keep_ref, recv_ref, own_ref, send_ref, term_ref):
    positive, log_total = totals((s0, s1, s2, s3))
    mine = jnp.exp(s0[0:1, :] - log_total)
    other = jnp.exp(s1[0:1, :] - log_total)
    own_ref[...] = keep_ref[:LANES, :] * mine + recv_ref[:LANES, :].astype(F32) * other
    send_ref[...] = (keep_ref[LANES:, :] * mine + recv_ref[LANES:, :].astype(F32) * other).astype(BF16)
    term_ref[...] = jnp.exp(positive - log_total) - 1.0


def items_kernel(s0, s1, s2, s3, e_ref, q_ref, out_ref, acc):
    step = pl.program_id(0)
    _, log_total = totals((s0, s1, s2, s3))
    weights = (e_ref[...] * jnp.exp(s0[0:1, :] - log_total)).astype(BF16)
    part = dot(weights, q_ref[...], 1, 0)

    @pl.when(step == 0)
    def _():
        acc[...] = part

    @pl.when(step > 0)
    def _():
        acc[...] += part

    @pl.when(step == pl.num_programs(0) - 1)
    def _():
        out_ref[...] = acc[...].astype(BF16)


def unpack_kernel(len_ref, own_ref, recv_ref, term_ref, pp_ref, out_ref, packed):
    rows = own_ref.shape[1]
    for k in range(rows // LANES):
        at = slice(k * LANES, (k + 1) * LANES)
        block = (own_ref[:, at] + recv_ref[:, at].astype(F32)).T
        term = jnp.broadcast_to(term_ref[:, at], (LANES, LANES)).T
        packed[at, :] = block + term * pp_ref[at, :].astype(F32)
    index = lax.broadcasted_iota(jnp.int32, (CHUNK, LANES), 0)
    start = jnp.int32(0)
    for h in range(len_ref.shape[1]):
        size = len_ref[0, h]
        for c in range(0, MAXLEN, CHUNK):
            at = slice(h * MAXLEN + c, h * MAXLEN + c + CHUNK)

            @pl.when(size > c)
            def _():
                out_ref[at, :] = jnp.where(index < size - c, packed[pl.ds(start + c, CHUNK), :], 0.0).astype(BF16)

            @pl.when(size <= c)
            def _():
                out_ref[at, :] = jnp.zeros((CHUNK, LANES), BF16)

        start = start + size


def swap(value, step, groups):
    return lax.ppermute(value, "grp", [(g, g ^ step) for g in range(groups)])


def shards(live, query, pos_emb, pos_ids, lengths, negatives, neg_ids):
    groups = lax.axis_size("grp")
    seqs = lax.axis_size("seq")
    own_neg, width = negatives.shape
    slots = query.shape[0]
    negs = own_neg * seqs
    sds = jax.ShapeDtypeStruct
    tile = min(512, live)
    steps = live // tile

    digits = jnp.stack([neg_ids // 65536, (neg_ids // 256) % 256, neg_ids % 256], axis=1).astype(BF16)
    row = jnp.concatenate([negatives, jnp.pad(digits, ((0, 0), (0, LANES - 3)))], axis=1)

    qp = pl.pallas_call(
        pack_query,
        out_shape=sds((live, LANES), BF16),
        in_specs=[small(), whole()],
        out_specs=whole(),
        scratch_shapes=[pltpu.VMEM((live + MAXLEN, LANES), F32)],
        compiler_params=params(),
        name="pack_query",
    )(lengths, query)
    q2 = swap(qp, 2, groups)
    q1 = swap(qp, 1, groups)
    q3 = swap(q2, 1, groups)

    pp, part, idp = pl.pallas_call(
        pack_positive,
        out_shape=(sds((live, LANES), BF16), sds((1, live), F32), sds((1, live), F32)),
        in_specs=[small(), whole(), whole(), whole()],
        out_specs=(whole(), whole(), whole()),
        scratch_shapes=[
            pltpu.VMEM((live + MAXLEN, LANES), F32),
            pltpu.VMEM((live // LANES + 8, LANES), jnp.int32),
        ],
        compiler_params=params(),
        name="pack_positive",
    )(lengths, pos_emb, pos_ids.reshape(slots // LANES, LANES), qp)

    pool = lax.all_to_all(jnp.tile(row, (seqs, 1)), "seq", split_axis=0, concat_axis=0, tiled=True)

    tall = pl.BlockSpec((tile, LANES), lambda i: (i, 0))
    line = pl.BlockSpec((1, tile), lambda i: (0, i))
    e_spec = pl.BlockSpec((negs, tile), lambda i: (0, i))
    stat_spec = pl.BlockSpec((4, tile), lambda i: (0, i))
    pool_spec = pl.BlockSpec((negs, width + LANES), lambda i: (0, 0))
    qfull, e, stat = pl.pallas_call(
        scores_kernel,
        grid=(steps,),
        out_shape=(sds((live, width), BF16), sds((negs, live), F32), sds((4, live), F32)),
        in_specs=[pool_spec, tall, tall, tall, tall, line, line],
        out_specs=(pl.BlockSpec((tile, width), lambda i: (i, 0)), e_spec, stat_spec),
        scratch_shapes=[pltpu.VMEM((negs, LANES), F32)],
        compiler_params=params(),
        name="scores",
    )(pool, qp, q1, q2, q3, idp, part)

    stats = (stat, swap(stat, 1, groups), swap(stat, 2, groups), swap(stat, 3, groups))

    keep, send = pl.pallas_call(
        rows_kernel,
        grid=(steps,),
        out_shape=(sds((2 * LANES, live), F32), sds((2 * LANES, live), BF16)),
        in_specs=[pool_spec, e_spec],
        out_specs=(pl.BlockSpec((2 * LANES, tile), lambda i: (0, i)), pl.BlockSpec((2 * LANES, tile), lambda i: (0, i))),
        scratch_shapes=[pltpu.VMEM((width, negs), BF16)],
        compiler_params=params(),
        name="row_products",
    )(pool, e)
    recv = swap(send, 1, groups)

    own, onward, term = pl.pallas_call(
        combine_kernel,
        out_shape=(sds((LANES, live), F32), sds((LANES, live), BF16), sds((1, live), F32)),
        in_specs=[whole()] * 6,
        out_specs=(whole(), whole(), whole()),
        compiler_params=params(),
        name="combine",
    )(*stats, keep, recv)
    recv2 = swap(onward, 2, groups)

    items = pl.pallas_call(
        items_kernel,
        grid=(steps,),
        out_shape=sds((negs, width), BF16),
        in_specs=[stat_spec] * 4 + [e_spec, pl.BlockSpec((tile, width), lambda i: (i, 0))],
        out_specs=pl.BlockSpec((negs, width), lambda i: (0, 0)),
        scratch_shapes=[pltpu.VMEM((negs, width), F32)],
        compiler_params=params(),
        name="item_products",
    )(*stats, e, qfull)
    shares = lax.all_to_all(items, "seq", split_axis=0, concat_axis=0, tiled=True)
    grad_items = jnp.sum(shares.reshape(seqs, own_neg, width).astype(F32), axis=0)

    grad_query = pl.pallas_call(
        unpack_kernel,
        out_shape=sds((slots, LANES), BF16),
        in_specs=[small()] + [whole()] * 4,
        out_specs=whole(),
        scratch_shapes=[pltpu.VMEM((live + MAXLEN, LANES), F32)],
        compiler_params=params(),
        name="unpack",
    )(lengths, own, recv2, term, pp)
    return grad_query, grad_items


def solution(mesh, live=2048):
    return jax.shard_map(
        partial(shards, live),
        mesh=mesh,
        in_specs=(
            P("seq", "grp"),
            P("seq", "grp"),
            P("seq"),
            P("seq", None),
            P(("seq", "grp"), None),
            P(("seq", "grp")),
        ),
        out_specs=(P("seq", "grp"), P(("seq", "grp"), None)),
        check_vma=False,
    )
```

```python
from functools import partial

import jax
import jax.numpy as jnp
from jax import lax
from jax.experimental import pallas as pl
from jax.experimental.pallas import tpu as pltpu
from jax.sharding import Mesh
from jax.sharding import PartitionSpec as P

MAXLEN = 192
LANES = 128
CHUNK = 64
TILE = 512
FLOOR = -1e30
MASKED = -3e38
SEQ = ("x", "zl", "y")
F32 = jnp.float32
BF16 = jnp.bfloat16
VMEM_BYTES = 14 * 1024 * 1024


def params():
    return pltpu.CompilerParams(vmem_limit_bytes=VMEM_BYTES)


def whole():
    return pl.BlockSpec(memory_space=pltpu.VMEM)


def small():
    return pl.BlockSpec(memory_space=pltpu.SMEM)


def dot(a, b, da, db):
    return lax.dot_general(a, b, (((da,), (db,)), ((), ())), preferred_element_type=F32)


def copy_rows(len_ref, src_ref, packed):
    start = jnp.int32(0)
    for h in range(len_ref.shape[1]):
        size = len_ref[0, h]
        for c in range(0, MAXLEN, CHUNK):

            @pl.when(size > c)
            def _():
                packed[pl.ds(start + c, CHUNK), :] = src_ref[h * MAXLEN + c : h * MAXLEN + c + CHUNK, :].astype(F32)

        start = start + size


def pass_on(value_ref, after_ref, out_ref):
    pass


def copies_kernel(row_ref, other_ref, out_ref):
    first = lax.axis_index("zl") == 0
    size = row_ref.shape[0]
    row, other = row_ref[...], other_ref[...]
    pair = (jnp.where(first, row, other), jnp.where(first, other, row))
    for i in range(out_ref.shape[0] // size):
        out_ref[i * size : (i + 1) * size, :] = pair[i % 2]


def sum_kernel(share_ref, after_ref, out_ref):
    size = out_ref.shape[0]
    total = share_ref[:size, :].astype(F32)
    for i in range(1, share_ref.shape[0] // size):
        total = total + share_ref[i * size : (i + 1) * size, :].astype(F32)
    out_ref[...] = total


def pack_query(len_ref, q_ref, qp_ref, packed):
    copy_rows(len_ref, q_ref, packed)
    qp_ref[...] = packed[: qp_ref.shape[0], :].astype(BF16)


def pack_positive(len_ref, p_ref, id_ref, qp_ref, pt_ref, part_ref, idp_ref, packed, ids):
    rows = qp_ref.shape[0]
    copy_rows(len_ref, p_ref, packed)
    ones = jnp.ones((16, LANES), BF16)
    for k in range(rows // LANES):
        at = slice(k * LANES, (k + 1) * LANES)
        held = packed[at, :]
        pt_ref[:, at] = held.T.astype(BF16)
        product = held * qp_ref[at, :].astype(F32)
        high = product.astype(BF16)
        low = (product - high.astype(F32)).astype(BF16)
        part_ref[:, at] = (dot(ones, high, 1, 1) + dot(ones, low, 1, 1))[:1, :]
    lane = lax.broadcasted_iota(jnp.int32, (1, LANES), 1)
    start = jnp.int32(0)
    for h in range(len_ref.shape[1]):
        row, off = divmod(h * MAXLEN, LANES)
        at = start + (LANES - off)
        target = at // LANES
        shift = at - target * LANES
        first = pltpu.roll(id_ref[row : row + 1, :], shift, 1)
        second = pltpu.roll(id_ref[row + 1 : row + 2, :], shift, 1)
        kept0 = ids[pl.ds(target, 1), :]
        kept1 = ids[pl.ds(target + 1, 1), :]
        ids[pl.ds(target, 1), :] = jnp.where(lane >= shift + off, first, kept0)
        ids[pl.ds(target + 1, 1), :] = jnp.where(
            lane + LANES >= shift + off, jnp.where(lane >= shift, second, first), kept1
        )
        ids[pl.ds(target + 2, 1), :] = second
        start = start + len_ref[0, h]
    for k in range(rows // LANES):
        idp_ref[:, k * LANES : (k + 1) * LANES] = ids[k + 1 : k + 2, :].astype(F32)


def block_of(order, step):
    return pl.ds(pl.multiple_of((order ^ step) * LANES, LANES), LANES)


def scores_kernel(neg_ref, q0_ref, q1_ref, q2_ref, q3_ref, idp_ref, part_ref, qfull_ref, e_ref, stat_ref, negid):
    member = lax.axis_index("grp")
    width = 4 * LANES
    lane = lax.broadcasted_iota(jnp.int32, (1, LANES), 1)
    place = jnp.where(lane == 0, 65536.0, jnp.where(lane == 1, 256.0, jnp.where(lane == 2, 1.0, 0.0)))
    value = jnp.sum(neg_ref[:, width : width + LANES].astype(F32) * place, axis=1, keepdims=True)
    negid[...] = jnp.broadcast_to(value, negid.shape)
    for t in range(0, qfull_ref.shape[0], TILE):
        rows = slice(t, t + TILE)
        for k, ref in enumerate((q0_ref, q1_ref, q2_ref, q3_ref)):
            qfull_ref[rows, block_of(member, k)] = ref[rows, :]
        scores = dot(neg_ref[:, :width], qfull_ref[rows, :], 1, 1)
        for k in range(TILE // LANES):
            at = slice(t + k * LANES, t + (k + 1) * LANES)
            part = jnp.where(negid[...] == idp_ref[:, at], MASKED, scores[:, k * LANES : (k + 1) * LANES])
            top = jnp.maximum(jnp.max(part, axis=0, keepdims=True), FLOOR)
            e = jnp.exp(part - top)
            e_ref[:, at] = e
            stat_ref[0:1, at] = top
            stat_ref[1:2, at] = jnp.sum(e, axis=0, keepdims=True)
    stat_ref[2:3, :] = part_ref[...]
    stat_ref[3:4, :] = part_ref[...]


def rows_kernel(neg_ref, e_ref, keep_ref, send_ref, turned):
    member = lax.axis_index("grp")
    half = 2 * LANES
    for k, step in enumerate((0, 2, 1, 3)):
        turned[k * LANES : (k + 1) * LANES, :] = neg_ref[:, block_of(member, step)].T
    for t in range(0, e_ref.shape[1], TILE):
        at = slice(t, t + TILE)
        out = dot(turned[...], e_ref[:, at].astype(BF16), 1, 0)
        keep_ref[:, at] = out[:half, :]
        send_ref[:, at] = out[half:, :].astype(BF16)


def combine_kernel(s0, s1, s2, s3, keep_ref, recv_ref, own_ref, send_ref, term_ref, scale_ref):
    refs = (s0, s1, s2, s3)
    positive = s0[2:3, :] + s1[2:3, :] + s2[2:3, :] + s3[2:3, :]
    top = positive
    for ref in refs:
        top = jnp.maximum(top, ref[0:1, :])
    total = jnp.exp(positive - top)
    for ref in refs:
        total = total + ref[1:2, :] * jnp.exp(ref[0:1, :] - top)
    log_total = top + jnp.log(total)
    mine = jnp.exp(s0[0:1, :] - log_total)
    other = jnp.exp(s1[0:1, :] - log_total)
    scale_ref[...] = mine
    term_ref[...] = jnp.exp(positive - log_total) - 1.0
    send_ref[...] = (keep_ref[LANES:, :] * mine + recv_ref[LANES:, :].astype(F32) * other).astype(BF16)
    own_ref[...] = keep_ref[:LANES, :] * mine + recv_ref[:LANES, :].astype(F32) * other


def items_kernel(scale_ref, e_ref, q_ref, out_ref):
    total = None
    for t in range(0, e_ref.shape[1], TILE):
        at = slice(t, t + TILE)
        weights = (e_ref[:, at] * scale_ref[:, at]).astype(BF16)
        part = dot(weights, q_ref[at, :], 1, 0)
        total = part if total is None else total + part
    x, y, z = lax.axis_size("x"), lax.axis_size("y"), lax.axis_size("zl")
    size = out_ref.shape[0] // (x * y * z)
    for i in range(x * y * z):
        src = ((i // (y * z)) * y + i % y) * z + (i // y) % z
        out_ref[i * size : (i + 1) * size, :] = total[src * size : (src + 1) * size, :].astype(BF16)


def unpack_kernel(len_ref, own_ref, recv_ref, term_ref, pt_ref, out_ref, packed):
    rows = own_ref.shape[1]
    for k in range(rows // LANES):
        at = slice(k * LANES, (k + 1) * LANES)
        packed[at, :] = (own_ref[:, at] + recv_ref[:, at].astype(F32) + term_ref[:, at] * pt_ref[:, at].astype(F32)).T
    index = lax.broadcasted_iota(jnp.int32, (CHUNK, LANES), 0)
    start = jnp.int32(0)
    for h in range(len_ref.shape[1]):
        size = len_ref[0, h]
        for c in range(0, MAXLEN, CHUNK):
            at = slice(h * MAXLEN + c, h * MAXLEN + c + CHUNK)

            @pl.when(size > c)
            def _():
                out_ref[at, :] = jnp.where(index < size - c, packed[pl.ds(start + c, CHUNK), :], 0.0).astype(BF16)

            @pl.when(size <= c)
            def _():
                out_ref[at, :] = jnp.zeros((CHUNK, LANES), BF16)

        start = start + size


def held(value):
    return pltpu.with_memory_space_constraint(value, pltpu.VMEM)


def after(value, other):
    any_place = pl.BlockSpec(memory_space=pl.ANY)
    return pl.pallas_call(
        pass_on,
        out_shape=pltpu.VMEM(value.shape, value.dtype),
        in_specs=[any_place, any_place],
        out_specs=any_place,
        input_output_aliases={0: 0},
        compiler_params=params(),
        name="after",
    )(held(value), other)


def swap(value, step, groups):
    return lax.ppermute(value, "grp", [(g, g ^ step) for g in range(groups)])


def shards(live, query, pos_emb, pos_ids, lengths, negatives, neg_ids):
    groups = lax.axis_size("grp")
    seqs = lax.axis_size(SEQ)
    near = lax.axis_size("zl")
    own_neg, width = negatives.shape
    slots = query.shape[0]
    negs = own_neg * seqs
    half = 2 * LANES
    vmem = pltpu.VMEM

    digits = jnp.stack([neg_ids // 65536, (neg_ids // 256) % 256, neg_ids % 256], axis=1).astype(BF16)
    row = jnp.concatenate([negatives, jnp.pad(digits, ((0, 0), (0, LANES - 3)))], axis=1)

    other = lax.ppermute(row, "zl", [(i, near - 1 - i) for i in range(near)])
    qp = pl.pallas_call(
        pack_query,
        out_shape=vmem((live, LANES), BF16),
        in_specs=[small(), whole()],
        out_specs=whole(),
        scratch_shapes=[vmem((live + MAXLEN, LANES), F32)],
        compiler_params=params(),
        name="pack_query",
    )(lengths, query)
    qp = after(qp, other)
    q2 = swap(qp, 2, groups)
    q1 = swap(qp, 1, groups)
    q3 = swap(q2, 1, groups)

    pt, part, idp = pl.pallas_call(
        pack_positive,
        out_shape=(vmem((LANES, live), BF16), vmem((1, live), F32), vmem((1, live), F32)),
        in_specs=[small(), whole(), whole(), whole()],
        out_specs=(whole(), whole(), whole()),
        scratch_shapes=[vmem((live + MAXLEN, LANES), F32), vmem((live // LANES + 8, LANES), jnp.int32)],
        compiler_params=params(),
        name="pack_positive",
    )(lengths, pos_emb, pos_ids.reshape(slots // LANES, LANES), held(qp))

    copies = pl.pallas_call(
        copies_kernel,
        out_shape=vmem((negs, width + LANES), BF16),
        in_specs=[whole()] * 2,
        out_specs=whole(),
        compiler_params=params(),
        name="copies",
    )(held(row), held(other))
    pool = lax.all_to_all(copies, ("x", "y"), split_axis=0, concat_axis=0, tiled=True)
    pool = held(pool)

    qfull, e, stat = pl.pallas_call(
        scores_kernel,
        out_shape=(vmem((live, width), BF16), vmem((negs, live), F32), vmem((4, live), F32)),
        in_specs=[whole()] * 7,
        out_specs=(whole(), whole(), whole()),
        scratch_shapes=[vmem((negs, LANES), F32)],
        compiler_params=params(),
        name="scores",
    )(pool, held(qp), held(q1), held(q2), held(q3), held(idp), held(part))
    stat2 = swap(stat, 2, groups)
    stats = [held(s) for s in (stat, swap(stat, 1, groups), stat2, swap(stat2, 1, groups))]

    keep, send = pl.pallas_call(
        rows_kernel,
        out_shape=(vmem((half, live), F32), vmem((half, live), BF16)),
        in_specs=[whole()] * 2,
        out_specs=(whole(), whole()),
        scratch_shapes=[vmem((width, negs), BF16)],
        compiler_params=params(),
        name="row_products",
    )(pool, held(e))
    recv = swap(send, 1, groups)

    own, onward, term, scale = pl.pallas_call(
        combine_kernel,
        out_shape=(vmem((LANES, live), F32), vmem((LANES, live), BF16), vmem((1, live), F32), vmem((1, live), F32)),
        in_specs=[whole()] * 6,
        out_specs=(whole(), whole(), whole(), whole()),
        compiler_params=params(),
        name="combine",
    )(*stats, held(keep), held(recv))
    recv2 = swap(onward, 2, groups)

    items = pl.pallas_call(
        items_kernel,
        out_shape=vmem((negs, width), BF16),
        in_specs=[whole()] * 3,
        out_specs=whole(),
        compiler_params=params(),
        name="item_products",
    )(held(scale), held(e), held(qfull))
    shares = lax.all_to_all(items, SEQ, split_axis=0, concat_axis=0, tiled=True)
    last = swap(recv2[:16, :LANES], 1, groups)
    grad_items = pl.pallas_call(
        sum_kernel,
        out_shape=jax.ShapeDtypeStruct((own_neg, width), F32),
        in_specs=[whole(), pl.BlockSpec(memory_space=pl.ANY)],
        out_specs=whole(),
        compiler_params=params(),
        name="sum_shares",
    )(shares, last)

    grad_query = pl.pallas_call(
        unpack_kernel,
        out_shape=jax.ShapeDtypeStruct((slots, LANES), BF16),
        in_specs=[small()] + [whole()] * 4,
        out_specs=whole(),
        scratch_shapes=[vmem((live + MAXLEN, LANES), F32)],
        compiler_params=params(),
        name="unpack",
    )(lengths, held(own), held(recv2), held(term), held(pt))
    return grad_query, grad_items


def solution(mesh, live=2048):
    split = Mesh(mesh.devices.reshape(4, 2, 4, mesh.shape["grp"]), SEQ + ("grp",))
    return jax.shard_map(
        partial(shards, live),
        mesh=split,
        in_specs=(
            P(SEQ, "grp"),
            P(SEQ, "grp"),
            P(SEQ),
            P(SEQ, None),
            P(SEQ + ("grp",), None),
            P(SEQ + ("grp",)),
        ),
        out_specs=(P(SEQ, "grp"), P(SEQ + ("grp",), None)),
        check_vma=False,
    )
```

```python
from functools import partial

import jax
import jax.numpy as jnp
from jax import lax
from jax.experimental import pallas as pl
from jax.experimental.pallas import tpu as pltpu
from jax.sharding import Mesh
from jax.sharding import PartitionSpec as P

MAXLEN = 192
LANES = 128
CHUNK = 64
TILE = 512
PARTS = 4
FLOOR = -1e30
MASKED = -3e38
SEQ = ("x", "zl", "y")
F32 = jnp.float32
BF16 = jnp.bfloat16
VMEM_BYTES = 14 * 1024 * 1024


def params():
    return pltpu.CompilerParams(vmem_limit_bytes=VMEM_BYTES)


def whole():
    return pl.BlockSpec(memory_space=pltpu.VMEM)


def anywhere():
    return pl.BlockSpec(memory_space=pl.ANY)


def small():
    return pl.BlockSpec(memory_space=pltpu.SMEM)


def dot(a, b, da, db):
    return lax.dot_general(a, b, (((da,), (db,)), ((), ())), preferred_element_type=F32)


def copy_rows(len_ref, src_ref, packed, first, last, start):
    for h in range(first, last):
        size = len_ref[0, h]
        for c in range(0, MAXLEN, CHUNK):

            @pl.when(size > c)
            def _():
                packed[pl.ds(start + c, CHUNK), :] = src_ref[h * MAXLEN + c : h * MAXLEN + c + CHUNK, :].astype(F32)

        start = start + size
    return start


def pass_on(value_ref, after_ref, out_ref):
    pass


def copies_kernel(row_ref, other_ref, out_ref):
    first = lax.axis_index("zl") == 0
    size = row_ref.shape[0]
    row, other = row_ref[...], other_ref[...]
    pair = (jnp.where(first, row, other), jnp.where(first, other, row))
    for i in range(out_ref.shape[0] // size):
        out_ref[i * size : (i + 1) * size, :] = pair[i % 2]


def sum_kernel(share_ref, own_ref, other_ref):
    first = lax.axis_index("zl") == 0
    size = own_ref.shape[0]
    totals = []
    for k in range(2):
        parts = [
            share_ref[i + k * size : i + (k + 1) * size, :].astype(F32)
            for i in range(0, share_ref.shape[0], 2 * size)
        ]
        while len(parts) > 1:
            parts = [a + b for a, b in zip(parts[::2], parts[1::2])]
        totals.append(parts[0])
    own_ref[...] = jnp.where(first, totals[0], totals[1])
    other_ref[...] = jnp.where(first, totals[1], totals[0])


def add_kernel(own_ref, recv_ref, out_ref):
    out_ref[...] = own_ref[...] + recv_ref[...]


def row_kernel(neg_ref, id_ref, out_ref, held_id, sems):
    rows, width = neg_ref.shape
    load_id = pltpu.make_async_copy(id_ref, held_id, sems.at[0])
    load = pltpu.make_async_copy(neg_ref, out_ref.at[:, pl.ds(0, width)], sems.at[1])
    load_id.start()
    load.start()
    load_id.wait()
    shape = (rows, LANES)
    lane = lax.broadcasted_iota(jnp.int32, shape, 1)
    ids = jnp.concatenate([held_id[...], jnp.zeros((1, LANES - rows), jnp.int32)], axis=1)
    own = lane == lax.broadcasted_iota(jnp.int32, shape, 0)
    value = jnp.sum(jnp.where(own, jnp.broadcast_to(ids, shape), 0), axis=1, keepdims=True)
    value = jnp.broadcast_to(value, shape)
    digit = jnp.where(lane == 0, value >> 16, jnp.where(lane == 1, (value >> 8) & 255, value & 255))
    out_ref[:, width:] = jnp.where(lane < 3, digit, 0).astype(F32).astype(BF16)
    load.wait()


def pack_query(len_ref, q_ref, qp_ref, held_q, held_len, packed, sems):
    parts = sems.shape[0] - 1
    size = q_ref.shape[0] // parts
    rows = [slice(i * size, (i + 1) * size) for i in range(parts)]
    loads = [pltpu.make_async_copy(q_ref.at[at], held_q.at[at], sems.at[i]) for i, at in enumerate(rows)]
    lengths = pltpu.make_async_copy(len_ref, held_len, sems.at[parts])
    lengths.start()
    for load in loads:
        load.start()
    lengths.wait()
    start = jnp.int32(0)
    per = size // MAXLEN
    for i, load in enumerate(loads):
        load.wait()
        start = copy_rows(held_len, held_q, packed, i * per, (i + 1) * per, start)
    qp_ref[...] = packed[: qp_ref.shape[0], :].astype(BF16)


def pack_positive(len_ref, p_ref, id_ref, qp_ref, pt_ref, part_ref, idp_ref, packed, ids):
    rows = qp_ref.shape[0]
    copy_rows(len_ref, p_ref, packed, 0, len_ref.shape[1], jnp.int32(0))
    ones = jnp.ones((16, LANES), BF16)
    for k in range(rows // LANES):
        at = slice(k * LANES, (k + 1) * LANES)
        held = packed[at, :]
        pt_ref[:, at] = held.T.astype(BF16)
        product = held * qp_ref[at, :].astype(F32)
        high = product.astype(BF16)
        low = (product - high.astype(F32)).astype(BF16)
        part_ref[:, at] = (dot(ones, high, 1, 1) + dot(ones, low, 1, 1))[:1, :]
    lane = lax.broadcasted_iota(jnp.int32, (1, LANES), 1)
    start = jnp.int32(0)
    for h in range(len_ref.shape[1]):
        row, off = divmod(h * MAXLEN, LANES)
        at = start + (LANES - off)
        target = at // LANES
        shift = at - target * LANES
        first = pltpu.roll(id_ref[row : row + 1, :], shift, 1)
        second = pltpu.roll(id_ref[row + 1 : row + 2, :], shift, 1)
        kept0 = ids[pl.ds(target, 1), :]
        kept1 = ids[pl.ds(target + 1, 1), :]
        ids[pl.ds(target, 1), :] = jnp.where(lane >= shift + off, first, kept0)
        ids[pl.ds(target + 1, 1), :] = jnp.where(
            lane + LANES >= shift + off, jnp.where(lane >= shift, second, first), kept1
        )
        ids[pl.ds(target + 2, 1), :] = second
        start = start + len_ref[0, h]
    for k in range(rows // LANES):
        idp_ref[:, k * LANES : (k + 1) * LANES] = ids[k + 1 : k + 2, :].astype(F32)


def block_of(order, step):
    return pl.ds(pl.multiple_of((order ^ step) * LANES, LANES), LANES)


def scores_kernel(neg_ref, q0_ref, q1_ref, q2_ref, q3_ref, idp_ref, part_ref, qfull_ref, e_ref, stat_ref, negid):
    member = lax.axis_index("grp")
    width = 4 * LANES
    lane = lax.broadcasted_iota(jnp.int32, (1, LANES), 1)
    place = jnp.where(lane == 0, 65536.0, jnp.where(lane == 1, 256.0, jnp.where(lane == 2, 1.0, 0.0)))
    value = jnp.sum(neg_ref[:, width : width + LANES].astype(F32) * place, axis=1, keepdims=True)
    negid[...] = jnp.broadcast_to(value, negid.shape)
    for k, ref in enumerate((q0_ref, q1_ref, q2_ref, q3_ref)):
        qfull_ref[:, block_of(member, k)] = ref[...]
    e_ref[...] = dot(neg_ref[:, :width], qfull_ref[...], 1, 1)
    for k in range(e_ref.shape[1] // LANES):
        at = slice(k * LANES, (k + 1) * LANES)
        part = jnp.where(negid[...] == idp_ref[:, at], MASKED, e_ref[:, at])
        top = jnp.maximum(jnp.max(part, axis=0, keepdims=True), FLOOR)
        e = jnp.exp(part - top)
        e_ref[:, at] = e
        stat_ref[0:1, at] = top
        stat_ref[1:2, at] = jnp.sum(e, axis=0, keepdims=True)
    stat_ref[2:3, :] = part_ref[...]
    stat_ref[3:4, :] = part_ref[...]


def rows_kernel(neg_ref, e_ref, keep_ref, send_ref, turned):
    member = lax.axis_index("grp")
    half = 2 * LANES
    for k, step in enumerate((0, 2, 1, 3)):
        turned[k * LANES : (k + 1) * LANES, :] = neg_ref[:, block_of(member, step)].T
    for t in range(0, e_ref.shape[1], TILE):
        at = slice(t, t + TILE)
        out = dot(turned[...], e_ref[:, at].astype(BF16), 1, 0)
        keep_ref[:, at] = out[:half, :]
        send_ref[:, at] = out[half:, :].astype(BF16)


def combine_kernel(s0, s1, s2, s3, keep_ref, recv_ref, own_ref, send_ref, term_ref, scale_ref):
    refs = (s0, s1, s2, s3)
    positive = s0[2:3, :] + s1[2:3, :] + s2[2:3, :] + s3[2:3, :]
    top = positive
    for ref in refs:
        top = jnp.maximum(top, ref[0:1, :])
    total = jnp.exp(positive - top)
    for ref in refs:
        total = total + ref[1:2, :] * jnp.exp(ref[0:1, :] - top)
    log_total = top + jnp.log(total)
    mine = jnp.exp(s0[0:1, :] - log_total)
    other = jnp.exp(s1[0:1, :] - log_total)
    scale_ref[...] = mine
    term_ref[...] = jnp.exp(positive - log_total) - 1.0
    send_ref[...] = (keep_ref[LANES:, :] * mine + recv_ref[LANES:, :].astype(F32) * other).astype(BF16)
    own_ref[...] = keep_ref[:LANES, :] * mine + recv_ref[:LANES, :].astype(F32) * other


def items_kernel(scale_ref, e_ref, q_ref, out_ref):
    total = None
    for t in range(0, e_ref.shape[1], TILE):
        at = slice(t, t + TILE)
        weights = (e_ref[:, at] * scale_ref[:, at]).astype(BF16)
        part = dot(weights, q_ref[at, :], 1, 0)
        total = part if total is None else total + part
    out_ref[...] = total.astype(BF16)


def unpack_kernel(len_ref, own_ref, recv_ref, term_ref, pt_ref, out_ref, packed, staged, sems):
    rows = own_ref.shape[1]
    for k in range(rows // LANES):
        at = slice(k * LANES, (k + 1) * LANES)
        packed[at, :] = (own_ref[:, at] + recv_ref[:, at].astype(F32) + term_ref[:, at] * pt_ref[:, at].astype(F32)).T
    index = lax.broadcasted_iota(jnp.int32, (CHUNK, LANES), 0)
    start = jnp.int32(0)
    parts = sems.shape[0]
    size = out_ref.shape[0] // parts
    stores = []
    for i in range(parts):
        for h in range(i * size // MAXLEN, (i + 1) * size // MAXLEN):
            count = len_ref[0, h]
            for c in range(0, MAXLEN, CHUNK):
                at = slice(h * MAXLEN + c, h * MAXLEN + c + CHUNK)

                @pl.when(count > c)
                def _():
                    live = jnp.where(index < count - c, packed[pl.ds(start + c, CHUNK), :], 0.0)
                    staged[at, :] = live.astype(BF16)

                @pl.when(count <= c)
                def _():
                    staged[at, :] = jnp.zeros((CHUNK, LANES), BF16)

            start = start + count
        at = slice(i * size, (i + 1) * size)
        stores.append(pltpu.make_async_copy(staged.at[at], out_ref.at[at], sems.at[i]))
        stores[-1].start()
    for store in stores:
        store.wait()


def held(value):
    return pltpu.with_memory_space_constraint(value, pltpu.VMEM)


def in_hbm(value):
    return pltpu.with_memory_space_constraint(value, pltpu.HBM)


def after(value, other):
    return pl.pallas_call(
        pass_on,
        out_shape=pltpu.VMEM(value.shape, value.dtype),
        in_specs=[anywhere()] * 2,
        out_specs=anywhere(),
        input_output_aliases={0: 0},
        compiler_params=params(),
        name="after",
    )(held(value), other)


def swap(value, step, groups):
    return lax.ppermute(value, "grp", [(g, g ^ step) for g in range(groups)])


def shards(live, query, pos_emb, pos_ids, lengths, negatives, neg_ids):
    groups = lax.axis_size("grp")
    seqs = lax.axis_size(SEQ)
    near = lax.axis_size("zl")
    own_neg, width = negatives.shape
    slots = query.shape[0]
    negs = own_neg * seqs
    half = 2 * LANES
    vmem = pltpu.VMEM

    row = pl.pallas_call(
        row_kernel,
        out_shape=vmem((own_neg, width + LANES), BF16),
        in_specs=[anywhere()] * 2,
        out_specs=whole(),
        scratch_shapes=[vmem((1, own_neg), jnp.int32), pltpu.SemaphoreType.DMA((2,))],
        compiler_params=params(),
        name="negative_rows",
    )(in_hbm(negatives), in_hbm(neg_ids.reshape(1, own_neg)))

    other = lax.ppermute(row, "zl", [(i, near - 1 - i) for i in range(near)])
    qp = pl.pallas_call(
        pack_query,
        out_shape=vmem((live, LANES), BF16),
        in_specs=[anywhere()] * 2,
        out_specs=whole(),
        scratch_shapes=[
            vmem((slots, LANES), BF16),
            pltpu.SMEM(lengths.shape, jnp.int32),
            vmem((live + MAXLEN, LANES), F32),
            pltpu.SemaphoreType.DMA((PARTS + 1,)),
        ],
        compiler_params=params(),
        name="pack_query",
    )(in_hbm(lengths), in_hbm(query))
    qp = after(qp, other)
    q2 = swap(qp, 2, groups)
    pt, part, idp = pl.pallas_call(
        pack_positive,
        out_shape=(jax.ShapeDtypeStruct((LANES, live), BF16), vmem((1, live), F32), vmem((1, live), F32)),
        in_specs=[small(), whole(), whole(), whole()],
        out_specs=(whole(), whole(), whole()),
        scratch_shapes=[vmem((live + MAXLEN, LANES), F32), vmem((live // LANES + 8, LANES), jnp.int32)],
        compiler_params=params(),
        name="pack_positive",
    )(lengths, pos_emb, pos_ids.reshape(slots // LANES, LANES), held(qp))

    q2 = after(q2, part)
    qp = after(qp, q2)
    q1 = swap(qp, 1, groups)
    q3 = swap(q2, 1, groups)

    copies = pl.pallas_call(
        copies_kernel,
        out_shape=vmem((negs, width + LANES), BF16),
        in_specs=[whole()] * 2,
        out_specs=whole(),
        compiler_params=params(),
        name="copies",
    )(held(row), held(other))
    pool = lax.all_to_all(copies, ("x", "y"), split_axis=0, concat_axis=0, tiled=True)
    pool = held(pool)

    qfull, e, stat = pl.pallas_call(
        scores_kernel,
        out_shape=(vmem((live, width), BF16), vmem((negs, live), F32), vmem((4, live), F32)),
        in_specs=[whole()] * 7,
        out_specs=(whole(), whole(), whole()),
        scratch_shapes=[vmem((negs, LANES), F32)],
        compiler_params=params(),
        name="scores",
    )(pool, held(qp), held(q1), held(q2), held(q3), held(idp), held(part))
    stat2 = swap(stat, 2, groups)
    stats = [held(s) for s in (stat, swap(stat, 1, groups), stat2, swap(stat2, 1, groups))]

    keep, send = pl.pallas_call(
        rows_kernel,
        out_shape=(vmem((half, live), F32), vmem((half, live), BF16)),
        in_specs=[whole()] * 2,
        out_specs=(whole(), whole()),
        scratch_shapes=[vmem((width, negs), BF16)],
        compiler_params=params(),
        name="row_products",
    )(pool, held(e))
    recv = swap(send, 1, groups)

    own, onward, term, scale = pl.pallas_call(
        combine_kernel,
        out_shape=(vmem((LANES, live), F32), vmem((LANES, live), BF16), vmem((1, live), F32), vmem((1, live), F32)),
        in_specs=[whole()] * 6,
        out_specs=(whole(), whole(), whole(), whole()),
        compiler_params=params(),
        name="combine",
    )(*stats, held(keep), held(recv))
    recv2 = swap(onward, 2, groups)

    items = pl.pallas_call(
        items_kernel,
        out_shape=vmem((negs, width), BF16),
        in_specs=[whole()] * 3,
        out_specs=whole(),
        compiler_params=params(),
        name="item_products",
    )(held(scale), held(e), held(qfull))
    shares = lax.all_to_all(items, ("x", "y"), split_axis=0, concat_axis=0, tiled=True)
    own_sum, other_sum = pl.pallas_call(
        sum_kernel,
        out_shape=(vmem((own_neg, width), F32), vmem((own_neg, width), F32)),
        in_specs=[whole()],
        out_specs=(whole(), whole()),
        compiler_params=params(),
        name="sum_shares",
    )(held(shares))
    other_sum = after(other_sum, recv2)
    recv_sum = lax.ppermute(other_sum, "zl", [(i, near - 1 - i) for i in range(near)])
    grad_items = pl.pallas_call(
        add_kernel,
        out_shape=jax.ShapeDtypeStruct((own_neg, width), F32),
        in_specs=[whole(), whole()],
        out_specs=whole(),
        compiler_params=params(),
        name="add_neighbour",
    )(held(own_sum), held(recv_sum))

    grad_query = pl.pallas_call(
        unpack_kernel,
        out_shape=jax.ShapeDtypeStruct((slots, LANES), BF16),
        in_specs=[small()] + [whole()] * 4,
        out_specs=anywhere(),
        scratch_shapes=[
            vmem((live + MAXLEN, LANES), F32),
            vmem((slots, LANES), BF16),
            pltpu.SemaphoreType.DMA((PARTS,)),
        ],
        compiler_params=params(),
        name="unpack",
    )(lengths, held(own), held(recv2), held(term), held(pt))
    return grad_query, grad_items


def solution(mesh, live=2048):
    split = Mesh(mesh.devices.reshape(4, 2, 4, mesh.shape["grp"]), SEQ + ("grp",))
    return jax.shard_map(
        partial(shards, live),
        mesh=split,
        in_specs=(
            P(SEQ, "grp"),
            P(SEQ, "grp"),
            P(SEQ),
            P(SEQ, None),
            P(SEQ + ("grp",), None),
            P(SEQ + ("grp",)),
        ),
        out_specs=(P(SEQ, "grp"), P(SEQ + ("grp",), None)),
        check_vma=False,
    )
```

```python
from functools import partial

import jax
import jax.numpy as jnp
from jax import lax
from jax.experimental import pallas as pl
from jax.experimental.pallas import tpu as pltpu
from jax.sharding import Mesh
from jax.sharding import PartitionSpec as P

MAXLEN = 192
LANES = 128
CHUNK = 64
TILE = 512
PARTS = 4
FLOOR = -1e30
MASKED = -3e38
SEQ = ("x", "zl", "y")
F32 = jnp.float32
BF16 = jnp.bfloat16
VMEM_BYTES = 14 * 1024 * 1024


def params():
    return pltpu.CompilerParams(vmem_limit_bytes=VMEM_BYTES)


def weight(micros):
    return pl.CostEstimate(flops=int(micros * 1e9), transcendentals=0, bytes_accessed=0)


def whole():
    return pl.BlockSpec(memory_space=pltpu.VMEM)


def anywhere():
    return pl.BlockSpec(memory_space=pl.ANY)


def small():
    return pl.BlockSpec(memory_space=pltpu.SMEM)


def dot(a, b, da, db):
    return lax.dot_general(a, b, (((da,), (db,)), ((), ())), preferred_element_type=F32)


def copy_rows(len_ref, src_ref, packed, first, last, start):
    for h in range(first, last):
        size = len_ref[0, h]
        for c in range(0, MAXLEN, CHUNK):

            @pl.when(size > c)
            def _():
                packed[pl.ds(start + c, CHUNK), :] = src_ref[h * MAXLEN + c : h * MAXLEN + c + CHUNK, :].astype(F32)

        start = start + size
    return start


def pass_on(value_ref, after_ref, out_ref):
    pass


def copies_kernel(row_ref, other_ref, out_ref):
    first = lax.axis_index("zl") == 0
    size = row_ref.shape[0]
    row, other = row_ref[...], other_ref[...]
    pair = (jnp.where(first, row, other), jnp.where(first, other, row))
    for i in range(out_ref.shape[0] // size):
        out_ref[i * size : (i + 1) * size, :] = pair[i % 2]


def sum_kernel(share_ref, own_ref, other_ref):
    first = lax.axis_index("zl") == 0
    size = own_ref.shape[0]
    totals = []
    for k in range(2):
        parts = [
            share_ref[i + k * size : i + (k + 1) * size, :].astype(F32)
            for i in range(0, share_ref.shape[0], 2 * size)
        ]
        while len(parts) > 1:
            parts = [a + b for a, b in zip(parts[::2], parts[1::2])]
        totals.append(parts[0])
    own_ref[...] = jnp.where(first, totals[0], totals[1])
    other_ref[...] = jnp.where(first, totals[1], totals[0])


def add_kernel(own_ref, recv_ref, out_ref):
    out_ref[...] = own_ref[...] + recv_ref[...]


def row_kernel(neg_ref, id_ref, out_ref, held_id, sems):
    rows, width = neg_ref.shape
    load_id = pltpu.make_async_copy(id_ref, held_id, sems.at[0])
    load = pltpu.make_async_copy(neg_ref, out_ref.at[:, pl.ds(0, width)], sems.at[1])
    load_id.start()
    load.start()
    load_id.wait()
    shape = (rows, LANES)
    lane = lax.broadcasted_iota(jnp.int32, shape, 1)
    ids = jnp.concatenate([held_id[...], jnp.zeros((1, LANES - rows), jnp.int32)], axis=1)
    own = lane == lax.broadcasted_iota(jnp.int32, shape, 0)
    value = jnp.sum(jnp.where(own, jnp.broadcast_to(ids, shape), 0), axis=1, keepdims=True)
    value = jnp.broadcast_to(value, shape)
    digit = jnp.where(lane == 0, value >> 16, jnp.where(lane == 1, (value >> 8) & 255, value & 255))
    out_ref[:, width:] = jnp.where(lane < 3, digit, 0).astype(F32).astype(BF16)
    load.wait()


def pack_query(len_ref, q_ref, qp_ref, held_q, held_len, packed, sems):
    parts = sems.shape[0] - 1
    size = q_ref.shape[0] // parts
    rows = [slice(i * size, (i + 1) * size) for i in range(parts)]
    loads = [pltpu.make_async_copy(q_ref.at[at], held_q.at[at], sems.at[i]) for i, at in enumerate(rows)]
    lengths = pltpu.make_async_copy(len_ref, held_len, sems.at[parts])
    lengths.start()
    for load in loads:
        load.start()
    lengths.wait()
    start = jnp.int32(0)
    per = size // MAXLEN
    for i, load in enumerate(loads):
        load.wait()
        start = copy_rows(held_len, held_q, packed, i * per, (i + 1) * per, start)
    qp_ref[...] = packed[: qp_ref.shape[0], :].astype(BF16)


def pack_positive(len_ref, p_ref, id_ref, qp_ref, pt_ref, part_ref, idp_ref, packed, ids):
    rows = qp_ref.shape[0]
    copy_rows(len_ref, p_ref, packed, 0, len_ref.shape[1], jnp.int32(0))
    ones = jnp.ones((16, LANES), BF16)
    for k in range(rows // LANES):
        at = slice(k * LANES, (k + 1) * LANES)
        held = packed[at, :]
        pt_ref[:, at] = held.T.astype(BF16)
        product = held * qp_ref[at, :].astype(F32)
        high = product.astype(BF16)
        low = (product - high.astype(F32)).astype(BF16)
        part_ref[:, at] = (dot(ones, high, 1, 1) + dot(ones, low, 1, 1))[:1, :]
    lane = lax.broadcasted_iota(jnp.int32, (1, LANES), 1)
    start = jnp.int32(0)
    for h in range(len_ref.shape[1]):
        row, off = divmod(h * MAXLEN, LANES)
        at = start + (LANES - off)
        target = at // LANES
        shift = at - target * LANES
        first = pltpu.roll(id_ref[row : row + 1, :], shift, 1)
        second = pltpu.roll(id_ref[row + 1 : row + 2, :], shift, 1)
        kept0 = ids[pl.ds(target, 1), :]
        kept1 = ids[pl.ds(target + 1, 1), :]
        ids[pl.ds(target, 1), :] = jnp.where(lane >= shift + off, first, kept0)
        ids[pl.ds(target + 1, 1), :] = jnp.where(
            lane + LANES >= shift + off, jnp.where(lane >= shift, second, first), kept1
        )
        ids[pl.ds(target + 2, 1), :] = second
        start = start + len_ref[0, h]
    for k in range(rows // LANES):
        idp_ref[:, k * LANES : (k + 1) * LANES] = ids[k + 1 : k + 2, :].astype(F32)


def block_of(order, step):
    return pl.ds(pl.multiple_of((order ^ step) * LANES, LANES), LANES)


def place_kernel(steps, *refs):
    member = lax.axis_index("grp")
    for step, ref in zip(steps, refs[:2]):
        refs[-1][:, block_of(member, step)] = ref[...]


def scores_kernel(neg_ref, qfull_ref, idp_ref, part_ref, e_ref, stat_ref, negid):
    width = 4 * LANES
    lane = lax.broadcasted_iota(jnp.int32, (1, LANES), 1)
    place = jnp.where(lane == 0, 65536.0, jnp.where(lane == 1, 256.0, jnp.where(lane == 2, 1.0, 0.0)))
    value = jnp.sum(neg_ref[:, width : width + LANES].astype(F32) * place, axis=1, keepdims=True)
    negid[...] = jnp.broadcast_to(value, negid.shape)
    e_ref[...] = dot(neg_ref[:, :width], qfull_ref[...], 1, 1)
    for k in range(e_ref.shape[1] // LANES):
        at = slice(k * LANES, (k + 1) * LANES)
        part = jnp.where(negid[...] == idp_ref[:, at], MASKED, e_ref[:, at])
        top = jnp.maximum(jnp.max(part, axis=0, keepdims=True), FLOOR)
        e = jnp.exp(part - top)
        e_ref[:, at] = e
        stat_ref[0:1, at] = top
        stat_ref[1:2, at] = jnp.sum(e, axis=0, keepdims=True)
    stat_ref[2:3, :] = part_ref[...]
    stat_ref[3:4, :] = part_ref[...]


def rows_kernel(neg_ref, e_ref, keep_ref, send_ref, turned):
    member = lax.axis_index("grp")
    half = 2 * LANES
    for k, step in enumerate((0, 2, 1, 3)):
        turned[k * LANES : (k + 1) * LANES, :] = neg_ref[:, block_of(member, step)].T
    for t in range(0, e_ref.shape[1], TILE):
        at = slice(t, t + TILE)
        out = dot(turned[...], e_ref[:, at].astype(BF16), 1, 0)
        keep_ref[:, at] = out[:half, :]
        send_ref[:, at] = out[half:, :].astype(BF16)


def norm_kernel(s0, s1, s2, s3, after_ref, scale_ref, other_ref, term_ref):
    refs = (s0, s1, s2, s3)
    positive = s0[2:3, :] + s1[2:3, :] + s2[2:3, :] + s3[2:3, :]
    top = positive
    for ref in refs:
        top = jnp.maximum(top, ref[0:1, :])
    total = jnp.exp(positive - top)
    for ref in refs:
        total = total + ref[1:2, :] * jnp.exp(ref[0:1, :] - top)
    log_total = top + jnp.log(total)
    scale_ref[...] = jnp.exp(s0[0:1, :] - log_total)
    other_ref[...] = jnp.exp(s1[0:1, :] - log_total)
    term_ref[...] = jnp.exp(positive - log_total) - 1.0


def combine_kernel(scale_ref, other_ref, keep_ref, recv_ref, after_ref, own_ref, send_ref):
    mine, other = scale_ref[...], other_ref[...]
    send_ref[...] = (keep_ref[LANES:, :] * mine + recv_ref[LANES:, :].astype(F32) * other).astype(BF16)
    own_ref[...] = keep_ref[:LANES, :] * mine + recv_ref[:LANES, :].astype(F32) * other


def items_kernel(scale_ref, e_ref, q_ref, out_ref):
    total = None
    for t in range(0, e_ref.shape[1], TILE):
        at = slice(t, t + TILE)
        weights = (e_ref[:, at] * scale_ref[:, at]).astype(BF16)
        part = dot(weights, q_ref[at, :], 1, 0)
        total = part if total is None else total + part
    out_ref[...] = total.astype(BF16)


def unpack_kernel(len_ref, own_ref, recv_ref, term_ref, pt_ref, out_ref, packed, staged, sems):
    rows = own_ref.shape[1]
    for k in range(rows // LANES):
        at = slice(k * LANES, (k + 1) * LANES)
        packed[at, :] = (own_ref[:, at] + recv_ref[:, at].astype(F32) + term_ref[:, at] * pt_ref[:, at].astype(F32)).T
    index = lax.broadcasted_iota(jnp.int32, (CHUNK, LANES), 0)
    start = jnp.int32(0)
    parts = sems.shape[0]
    size = out_ref.shape[0] // parts
    stores = []
    for i in range(parts):
        for h in range(i * size // MAXLEN, (i + 1) * size // MAXLEN):
            count = len_ref[0, h]
            for c in range(0, MAXLEN, CHUNK):
                at = slice(h * MAXLEN + c, h * MAXLEN + c + CHUNK)

                @pl.when(count > c)
                def _():
                    live = jnp.where(index < count - c, packed[pl.ds(start + c, CHUNK), :], 0.0)
                    staged[at, :] = live.astype(BF16)

                @pl.when(count <= c)
                def _():
                    staged[at, :] = jnp.zeros((CHUNK, LANES), BF16)

            start = start + count
        at = slice(i * size, (i + 1) * size)
        stores.append(pltpu.make_async_copy(staged.at[at], out_ref.at[at], sems.at[i]))
        stores[-1].start()
    for store in stores:
        store.wait()


def held(value):
    return pltpu.with_memory_space_constraint(value, pltpu.VMEM)


def in_hbm(value):
    return pltpu.with_memory_space_constraint(value, pltpu.HBM)


def after(value, other):
    return pl.pallas_call(
        pass_on,
        out_shape=pltpu.VMEM(value.shape, value.dtype),
        in_specs=[anywhere()] * 2,
        out_specs=anywhere(),
        input_output_aliases={0: 0},
        compiler_params=params(),
        name="after",
    )(held(value), other)


def swap(value, step, groups):
    return lax.ppermute(value, "grp", [(g, g ^ step) for g in range(groups)])


def shards(live, query, pos_emb, pos_ids, lengths, negatives, neg_ids):
    groups = lax.axis_size("grp")
    seqs = lax.axis_size(SEQ)
    near = lax.axis_size("zl")
    own_neg, width = negatives.shape
    slots = query.shape[0]
    negs = own_neg * seqs
    half = 2 * LANES
    vmem = pltpu.VMEM

    row = pl.pallas_call(
        row_kernel,
        out_shape=vmem((own_neg, width + LANES), BF16),
        in_specs=[anywhere()] * 2,
        out_specs=whole(),
        scratch_shapes=[vmem((1, own_neg), jnp.int32), pltpu.SemaphoreType.DMA((2,))],
        compiler_params=params(),
        name="negative_rows",
    )(in_hbm(negatives), in_hbm(neg_ids.reshape(1, own_neg)))

    other = lax.ppermute(row, "zl", [(i, near - 1 - i) for i in range(near)])
    qp = pl.pallas_call(
        pack_query,
        out_shape=vmem((live, LANES), BF16),
        in_specs=[anywhere()] * 2,
        out_specs=whole(),
        scratch_shapes=[
            vmem((slots, LANES), BF16),
            pltpu.SMEM(lengths.shape, jnp.int32),
            vmem((live + MAXLEN, LANES), F32),
            pltpu.SemaphoreType.DMA((PARTS + 1,)),
        ],
        compiler_params=params(),
        name="pack_query",
    )(in_hbm(lengths), in_hbm(query))
    qp = after(qp, other)
    q2 = swap(qp, 2, groups)
    pt, part, idp = pl.pallas_call(
        pack_positive,
        out_shape=(jax.ShapeDtypeStruct((LANES, live), BF16), vmem((1, live), F32), vmem((1, live), F32)),
        in_specs=[small(), whole(), whole(), whole()],
        out_specs=(whole(), whole(), whole()),
        scratch_shapes=[vmem((live + MAXLEN, LANES), F32), vmem((live // LANES + 8, LANES), jnp.int32)],
        compiler_params=params(),
        name="pack_positive",
    )(lengths, pos_emb, pos_ids.reshape(slots // LANES, LANES), held(qp))

    q2 = after(q2, part)
    qp = after(qp, q2)
    q1 = swap(qp, 1, groups)
    q3 = swap(q2, 1, groups)

    copies = pl.pallas_call(
        copies_kernel,
        out_shape=vmem((negs, width + LANES), BF16),
        in_specs=[whole()] * 2,
        out_specs=whole(),
        compiler_params=params(),
        name="copies",
    )(held(row), held(other))
    pool = lax.all_to_all(copies, ("x", "y"), split_axis=0, concat_axis=0, tiled=True)
    pool = held(pool)

    qfull = pl.pallas_call(
        partial(place_kernel, (0, 2)),
        out_shape=vmem((live, width), BF16),
        in_specs=[whole()] * 2,
        out_specs=whole(),
        compiler_params=params(),
        name="place_own",
    )(held(qp), held(q2))
    qfull = pl.pallas_call(
        partial(place_kernel, (1, 3)),
        out_shape=vmem((live, width), BF16),
        in_specs=[whole()] * 3,
        out_specs=whole(),
        input_output_aliases={2: 0},
        compiler_params=params(),
        name="place_near",
    )(held(q1), held(q3), held(qfull))
    qfull = held(qfull)
    e, stat = pl.pallas_call(
        scores_kernel,
        out_shape=(vmem((negs, live), F32), vmem((4, live), F32)),
        in_specs=[whole()] * 4,
        out_specs=(whole(), whole()),
        scratch_shapes=[vmem((negs, LANES), F32)],
        compiler_params=params(),
        name="scores",
    )(pool, qfull, held(idp), held(part))
    stats = [held(s) for s in (stat, swap(stat, 1, groups), swap(stat, 2, groups), swap(stat, 3, groups))]

    keep, send = pl.pallas_call(
        rows_kernel,
        out_shape=(vmem((half, live), F32), vmem((half, live), BF16)),
        in_specs=[whole()] * 2,
        out_specs=(whole(), whole()),
        scratch_shapes=[vmem((width, negs), BF16)],
        compiler_params=params(),
        name="row_products",
    )(pool, held(e))
    recv = swap(send, 1, groups)

    scale, other_scale, term = pl.pallas_call(
        norm_kernel,
        out_shape=(vmem((1, live), F32),) * 3,
        in_specs=[whole()] * 4 + [anywhere()],
        out_specs=(whole(),) * 3,
        compiler_params=params(),
        name="norm",
    )(*stats, keep)
    items = pl.pallas_call(
        items_kernel,
        out_shape=vmem((negs, width), BF16),
        in_specs=[whole()] * 3,
        out_specs=whole(),
        cost_estimate=weight(50),
        compiler_params=params(),
        name="item_products",
    )(held(scale), held(e), qfull)
    own, onward = pl.pallas_call(
        combine_kernel,
        out_shape=(vmem((LANES, live), F32), vmem((LANES, live), BF16)),
        in_specs=[whole()] * 4 + [anywhere()],
        out_specs=(whole(), whole()),
        compiler_params=params(),
        name="combine",
    )(held(scale), held(other_scale), held(keep), held(recv), items)
    recv2 = swap(onward, 2, groups)

    shares = lax.all_to_all(items, ("x", "y"), split_axis=0, concat_axis=0, tiled=True)
    own_sum, other_sum = pl.pallas_call(
        sum_kernel,
        out_shape=(vmem((own_neg, width), F32), vmem((own_neg, width), F32)),
        in_specs=[whole()],
        out_specs=(whole(), whole()),
        compiler_params=params(),
        name="sum_shares",
    )(held(shares))
    other_sum = after(other_sum, recv2)
    recv_sum = lax.ppermute(other_sum, "zl", [(i, near - 1 - i) for i in range(near)])
    grad_items = pl.pallas_call(
        add_kernel,
        out_shape=jax.ShapeDtypeStruct((own_neg, width), F32),
        in_specs=[whole(), whole()],
        out_specs=whole(),
        compiler_params=params(),
        name="add_neighbour",
    )(held(own_sum), held(recv_sum))

    grad_query = pl.pallas_call(
        unpack_kernel,
        out_shape=jax.ShapeDtypeStruct((slots, LANES), BF16),
        in_specs=[small()] + [whole()] * 4,
        out_specs=anywhere(),
        scratch_shapes=[
            vmem((live + MAXLEN, LANES), F32),
            vmem((slots, LANES), BF16),
            pltpu.SemaphoreType.DMA((PARTS,)),
        ],
        compiler_params=params(),
        name="unpack",
    )(lengths, held(own), held(recv2), held(term), held(pt))
    return grad_query, grad_items


def solution(mesh, live=2048):
    split = Mesh(mesh.devices.reshape(4, 2, 4, mesh.shape["grp"]), SEQ + ("grp",))
    return jax.shard_map(
        partial(shards, live),
        mesh=split,
        in_specs=(
            P(SEQ, "grp"),
            P(SEQ, "grp"),
            P(SEQ),
            P(SEQ, None),
            P(SEQ + ("grp",), None),
            P(SEQ + ("grp",)),
        ),
        out_specs=(P(SEQ, "grp"), P(SEQ + ("grp",), None)),
        check_vma=False,
    )
```

```python
from functools import partial

import jax
import jax.numpy as jnp
from jax import lax
from jax.experimental import pallas as pl
from jax.experimental.pallas import tpu as pltpu
from jax.sharding import Mesh
from jax.sharding import PartitionSpec as P

MAXLEN = 192
LANES = 128
CHUNK = 64
TILE = 512
PARTS = 4
FLOOR = -1e30
MASKED = -3e38
SEQ = ("x", "zl", "y")
F32 = jnp.float32
BF16 = jnp.bfloat16
VMEM_BYTES = 14 * 1024 * 1024


def params():
    return pltpu.CompilerParams(vmem_limit_bytes=VMEM_BYTES)


def weight(micros):
    return pl.CostEstimate(flops=int(micros * 1e9), transcendentals=0, bytes_accessed=0)


def whole():
    return pl.BlockSpec(memory_space=pltpu.VMEM)


def anywhere():
    return pl.BlockSpec(memory_space=pl.ANY)


def small():
    return pl.BlockSpec(memory_space=pltpu.SMEM)


def dot(a, b, da, db):
    return lax.dot_general(a, b, (((da,), (db,)), ((), ())), preferred_element_type=F32)


def copy_rows(len_ref, src_ref, packed, first, last, start):
    for h in range(first, last):
        size = len_ref[0, h]
        for c in range(0, MAXLEN, CHUNK):

            @pl.when(size > c)
            def _():
                packed[pl.ds(start + c, CHUNK), :] = src_ref[h * MAXLEN + c : h * MAXLEN + c + CHUNK, :].astype(F32)

        start = start + size
    return start


def pass_on(value_ref, after_ref, out_ref):
    pass


def copies_kernel(row_ref, other_ref, out_ref):
    first = lax.axis_index("zl") == 0
    size = row_ref.shape[0]
    row, other = row_ref[...], other_ref[...]
    pair = (jnp.where(first, row, other), jnp.where(first, other, row))
    for i in range(out_ref.shape[0] // size):
        out_ref[i * size : (i + 1) * size, :] = pair[i % 2]


def sum_kernel(share_ref, own_ref, other_ref):
    first = lax.axis_index("zl") == 0
    size = own_ref.shape[0]
    totals = []
    for k in range(2):
        parts = [
            share_ref[i + k * size : i + (k + 1) * size, :].astype(F32)
            for i in range(0, share_ref.shape[0], 2 * size)
        ]
        while len(parts) > 1:
            parts = [a + b for a, b in zip(parts[::2], parts[1::2])]
        totals.append(parts[0])
    own_ref[...] = jnp.where(first, totals[0], totals[1])
    other_ref[...] = jnp.where(first, totals[1], totals[0])


def add_kernel(own_ref, recv_ref, out_ref):
    out_ref[...] = own_ref[...] + recv_ref[...]


def row_kernel(neg_ref, id_ref, out_ref, held_id, sems):
    rows, width = neg_ref.shape
    load_id = pltpu.make_async_copy(id_ref, held_id, sems.at[0])
    load = pltpu.make_async_copy(neg_ref, out_ref.at[:, pl.ds(0, width)], sems.at[1])
    load_id.start()
    load.start()
    load_id.wait()
    shape = (rows, LANES)
    lane = lax.broadcasted_iota(jnp.int32, shape, 1)
    ids = jnp.concatenate([held_id[...], jnp.zeros((1, LANES - rows), jnp.int32)], axis=1)
    own = lane == lax.broadcasted_iota(jnp.int32, shape, 0)
    value = jnp.sum(jnp.where(own, jnp.broadcast_to(ids, shape), 0), axis=1, keepdims=True)
    value = jnp.broadcast_to(value, shape)
    digit = jnp.where(lane == 0, value >> 16, jnp.where(lane == 1, (value >> 8) & 255, value & 255))
    out_ref[:, width:] = jnp.where(lane < 3, digit, 0).astype(F32).astype(BF16)
    load.wait()


def pack_query(len_ref, q_ref, qp_ref, held_q, held_len, packed, sems):
    parts = sems.shape[0] - 1
    size = q_ref.shape[0] // parts
    rows = [slice(i * size, (i + 1) * size) for i in range(parts)]
    loads = [pltpu.make_async_copy(q_ref.at[at], held_q.at[at], sems.at[i]) for i, at in enumerate(rows)]
    lengths = pltpu.make_async_copy(len_ref, held_len, sems.at[parts])
    lengths.start()
    for load in loads:
        load.start()
    lengths.wait()
    start = jnp.int32(0)
    per = size // MAXLEN
    for i, load in enumerate(loads):
        load.wait()
        start = copy_rows(held_len, held_q, packed, i * per, (i + 1) * per, start)
    qp_ref[...] = packed[: qp_ref.shape[0], :].astype(BF16)


def pack_positive(len_ref, p_ref, id_ref, qp_ref, pt_ref, part_ref, idp_ref, packed, ids):
    rows = qp_ref.shape[0]
    copy_rows(len_ref, p_ref, packed, 0, len_ref.shape[1], jnp.int32(0))
    ones = jnp.ones((16, LANES), BF16)
    for k in range(rows // LANES):
        at = slice(k * LANES, (k + 1) * LANES)
        held = packed[at, :]
        pt_ref[:, at] = held.T.astype(BF16)
        product = held * qp_ref[at, :].astype(F32)
        high = product.astype(BF16)
        low = (product - high.astype(F32)).astype(BF16)
        part_ref[:, at] = (dot(ones, high, 1, 1) + dot(ones, low, 1, 1))[:1, :]
    lane = lax.broadcasted_iota(jnp.int32, (1, LANES), 1)
    start = jnp.int32(0)
    for h in range(len_ref.shape[1]):
        row, off = divmod(h * MAXLEN, LANES)
        at = start + (LANES - off)
        target = at // LANES
        shift = at - target * LANES
        first = pltpu.roll(id_ref[row : row + 1, :], shift, 1)
        second = pltpu.roll(id_ref[row + 1 : row + 2, :], shift, 1)
        kept0 = ids[pl.ds(target, 1), :]
        kept1 = ids[pl.ds(target + 1, 1), :]
        ids[pl.ds(target, 1), :] = jnp.where(lane >= shift + off, first, kept0)
        ids[pl.ds(target + 1, 1), :] = jnp.where(
            lane + LANES >= shift + off, jnp.where(lane >= shift, second, first), kept1
        )
        ids[pl.ds(target + 2, 1), :] = second
        start = start + len_ref[0, h]
    for k in range(rows // LANES):
        idp_ref[:, k * LANES : (k + 1) * LANES] = ids[k + 1 : k + 2, :].astype(F32)


def block_of(order, step):
    return pl.ds(pl.multiple_of((order ^ step) * LANES, LANES), LANES)


def place_kernel(steps, *refs):
    member = lax.axis_index("grp")
    for step, ref in zip(steps, refs[:2]):
        refs[-1][:, block_of(member, step)] = ref[...]


def scores_kernel(neg_ref, qfull_ref, idp_ref, part_ref, e_ref, stat_ref, negid):
    width = 4 * LANES
    lane = lax.broadcasted_iota(jnp.int32, (1, LANES), 1)
    place = jnp.where(lane == 0, 65536.0, jnp.where(lane == 1, 256.0, jnp.where(lane == 2, 1.0, 0.0)))
    value = jnp.sum(neg_ref[:, width : width + LANES].astype(F32) * place, axis=1, keepdims=True)
    negid[...] = jnp.broadcast_to(value, negid.shape)
    e_ref[...] = dot(neg_ref[:, :width], qfull_ref[...], 1, 1)
    for k in range(e_ref.shape[1] // LANES):
        at = slice(k * LANES, (k + 1) * LANES)
        part = jnp.where(negid[...] == idp_ref[:, at], MASKED, e_ref[:, at])
        top = jnp.maximum(jnp.max(part, axis=0, keepdims=True), FLOOR)
        e = jnp.exp(part - top)
        e_ref[:, at] = e
        stat_ref[0:1, at] = top
        stat_ref[1:2, at] = jnp.sum(e, axis=0, keepdims=True)
    stat_ref[2:3, :] = part_ref[...]
    stat_ref[3:4, :] = part_ref[...]


def rows_kernel(neg_ref, e_ref, keep_ref, send_ref, turned):
    member = lax.axis_index("grp")
    half = 2 * LANES
    for k, step in enumerate((0, 2, 1, 3)):
        turned[k * LANES : (k + 1) * LANES, :] = neg_ref[:, block_of(member, step)].T
    for t in range(0, e_ref.shape[1], TILE):
        at = slice(t, t + TILE)
        out = dot(turned[...], e_ref[:, at].astype(BF16), 1, 0)
        keep_ref[:, at] = out[:half, :]
        send_ref[:, at] = out[half:, :].astype(BF16)


def merge_kernel(own_ref, other_ref, out_ref):
    top = jnp.maximum(own_ref[0:1, :], other_ref[0:1, :])
    total = own_ref[1:2, :] * jnp.exp(own_ref[0:1, :] - top) + other_ref[1:2, :] * jnp.exp(other_ref[0:1, :] - top)
    out_ref[0:1, :] = top
    out_ref[1:2, :] = total
    out_ref[2:3, :] = own_ref[2:3, :] + other_ref[2:3, :]
    out_ref[3:4, :] = total


def norm_kernel(s0, s1, near, far, after_ref, scale_ref, other_ref, term_ref):
    positive = near[2:3, :] + far[2:3, :]
    top = jnp.maximum(jnp.maximum(near[0:1, :], far[0:1, :]), positive)
    total = jnp.exp(positive - top)
    for ref in (near, far):
        total = total + ref[1:2, :] * jnp.exp(ref[0:1, :] - top)
    log_total = top + jnp.log(total)
    scale_ref[...] = jnp.exp(s0[0:1, :] - log_total)
    other_ref[...] = jnp.exp(s1[0:1, :] - log_total)
    term_ref[...] = jnp.exp(positive - log_total) - 1.0


def combine_kernel(scale_ref, other_ref, keep_ref, recv_ref, after_ref, own_ref, send_ref):
    mine, other = scale_ref[...], other_ref[...]
    send_ref[...] = (keep_ref[LANES:, :] * mine + recv_ref[LANES:, :].astype(F32) * other).astype(BF16)
    own_ref[...] = keep_ref[:LANES, :] * mine + recv_ref[:LANES, :].astype(F32) * other


def items_kernel(scale_ref, e_ref, q_ref, out_ref):
    total = None
    for t in range(0, e_ref.shape[1], TILE):
        at = slice(t, t + TILE)
        weights = (e_ref[:, at] * scale_ref[:, at]).astype(BF16)
        part = dot(weights, q_ref[at, :], 1, 0)
        total = part if total is None else total + part
    out_ref[...] = total.astype(BF16)


def unpack_kernel(len_ref, own_ref, recv_ref, term_ref, pt_ref, out_ref, packed, staged, sems):
    rows = own_ref.shape[1]
    for k in range(rows // LANES):
        at = slice(k * LANES, (k + 1) * LANES)
        packed[at, :] = (own_ref[:, at] + recv_ref[:, at].astype(F32) + term_ref[:, at] * pt_ref[:, at].astype(F32)).T
    index = lax.broadcasted_iota(jnp.int32, (CHUNK, LANES), 0)
    start = jnp.int32(0)
    parts = sems.shape[0]
    size = out_ref.shape[0] // parts
    stores = []
    for i in range(parts):
        for h in range(i * size // MAXLEN, (i + 1) * size // MAXLEN):
            count = len_ref[0, h]
            for c in range(0, MAXLEN, CHUNK):
                at = slice(h * MAXLEN + c, h * MAXLEN + c + CHUNK)

                @pl.when(count > c)
                def _():
                    live = jnp.where(index < count - c, packed[pl.ds(start + c, CHUNK), :], 0.0)
                    staged[at, :] = live.astype(BF16)

                @pl.when(count <= c)
                def _():
                    staged[at, :] = jnp.zeros((CHUNK, LANES), BF16)

            start = start + count
        at = slice(i * size, (i + 1) * size)
        stores.append(pltpu.make_async_copy(staged.at[at], out_ref.at[at], sems.at[i]))
        stores[-1].start()
    for store in stores:
        store.wait()


def held(value):
    return pltpu.with_memory_space_constraint(value, pltpu.VMEM)


def in_hbm(value):
    return pltpu.with_memory_space_constraint(value, pltpu.HBM)


def after(value, other):
    return pl.pallas_call(
        pass_on,
        out_shape=pltpu.VMEM(value.shape, value.dtype),
        in_specs=[anywhere()] * 2,
        out_specs=anywhere(),
        input_output_aliases={0: 0},
        compiler_params=params(),
        name="after",
    )(held(value), other)


def swap(value, step, groups):
    return lax.ppermute(value, "grp", [(g, g ^ step) for g in range(groups)])


def shards(live, query, pos_emb, pos_ids, lengths, negatives, neg_ids):
    groups = lax.axis_size("grp")
    seqs = lax.axis_size(SEQ)
    near = lax.axis_size("zl")
    own_neg, width = negatives.shape
    slots = query.shape[0]
    negs = own_neg * seqs
    half = 2 * LANES
    vmem = pltpu.VMEM

    row = pl.pallas_call(
        row_kernel,
        out_shape=vmem((own_neg, width + LANES), BF16),
        in_specs=[anywhere()] * 2,
        out_specs=whole(),
        scratch_shapes=[vmem((1, own_neg), jnp.int32), pltpu.SemaphoreType.DMA((2,))],
        compiler_params=params(),
        name="negative_rows",
    )(in_hbm(negatives), in_hbm(neg_ids.reshape(1, own_neg)))

    other = lax.ppermute(row, "zl", [(i, near - 1 - i) for i in range(near)])
    qp = pl.pallas_call(
        pack_query,
        out_shape=vmem((live, LANES), BF16),
        in_specs=[anywhere()] * 2,
        out_specs=whole(),
        scratch_shapes=[
            vmem((slots, LANES), BF16),
            pltpu.SMEM(lengths.shape, jnp.int32),
            vmem((live + MAXLEN, LANES), F32),
            pltpu.SemaphoreType.DMA((PARTS + 1,)),
        ],
        compiler_params=params(),
        name="pack_query",
    )(in_hbm(lengths), in_hbm(query))
    qp = after(qp, other)
    q2 = swap(qp, 2, groups)
    pt, part, idp = pl.pallas_call(
        pack_positive,
        out_shape=(jax.ShapeDtypeStruct((LANES, live), BF16), vmem((1, live), F32), vmem((1, live), F32)),
        in_specs=[small(), whole(), whole(), whole()],
        out_specs=(whole(), whole(), whole()),
        scratch_shapes=[vmem((live + MAXLEN, LANES), F32), vmem((live // LANES + 8, LANES), jnp.int32)],
        compiler_params=params(),
        name="pack_positive",
    )(lengths, pos_emb, pos_ids.reshape(slots // LANES, LANES), held(qp))

    q2 = after(q2, part)
    qp = after(qp, q2)
    q1 = swap(qp, 1, groups)
    q3 = swap(q2, 1, groups)

    copies = pl.pallas_call(
        copies_kernel,
        out_shape=vmem((negs, width + LANES), BF16),
        in_specs=[whole()] * 2,
        out_specs=whole(),
        compiler_params=params(),
        name="copies",
    )(held(row), held(other))
    pool = lax.all_to_all(copies, ("x", "y"), split_axis=0, concat_axis=0, tiled=True)
    pool = held(pool)

    qfull = pl.pallas_call(
        partial(place_kernel, (0, 2)),
        out_shape=vmem((live, width), BF16),
        in_specs=[whole()] * 2,
        out_specs=whole(),
        compiler_params=params(),
        name="place_own",
    )(held(qp), held(q2))
    qfull = pl.pallas_call(
        partial(place_kernel, (1, 3)),
        out_shape=vmem((live, width), BF16),
        in_specs=[whole()] * 3,
        out_specs=whole(),
        input_output_aliases={2: 0},
        compiler_params=params(),
        name="place_near",
    )(held(q1), held(q3), held(qfull))
    qfull = held(qfull)
    e, stat = pl.pallas_call(
        scores_kernel,
        out_shape=(vmem((negs, live), F32), vmem((4, live), F32)),
        in_specs=[whole()] * 4,
        out_specs=(whole(), whole()),
        scratch_shapes=[vmem((negs, LANES), F32)],
        compiler_params=params(),
        name="scores",
    )(pool, qfull, held(idp), held(part))
    stat, stat1 = held(stat), held(swap(stat, 1, groups))
    near_stat = pl.pallas_call(
        merge_kernel,
        out_shape=vmem((4, live), F32),
        in_specs=[whole()] * 2,
        out_specs=whole(),
        compiler_params=params(),
        name="merge_stats",
    )(stat, stat1)
    stats = (stat, stat1, held(near_stat), held(swap(near_stat, 2, groups)))

    keep, send = pl.pallas_call(
        rows_kernel,
        out_shape=(vmem((half, live), F32), vmem((half, live), BF16)),
        in_specs=[whole()] * 2,
        out_specs=(whole(), whole()),
        scratch_shapes=[vmem((width, negs), BF16)],
        compiler_params=params(),
        name="row_products",
    )(pool, held(e))
    recv = swap(send, 1, groups)

    scale, other_scale, term = pl.pallas_call(
        norm_kernel,
        out_shape=(vmem((1, live), F32),) * 3,
        in_specs=[whole()] * 4 + [anywhere()],
        out_specs=(whole(),) * 3,
        compiler_params=params(),
        name="norm",
    )(*stats, keep)
    items = pl.pallas_call(
        items_kernel,
        out_shape=vmem((negs, width), BF16),
        in_specs=[whole()] * 3,
        out_specs=whole(),
        cost_estimate=weight(50),
        compiler_params=params(),
        name="item_products",
    )(held(scale), held(e), qfull)
    own, onward = pl.pallas_call(
        combine_kernel,
        out_shape=(vmem((LANES, live), F32), vmem((LANES, live), BF16)),
        in_specs=[whole()] * 4 + [anywhere()],
        out_specs=(whole(), whole()),
        compiler_params=params(),
        name="combine",
    )(held(scale), held(other_scale), held(keep), held(recv), items)
    recv2 = swap(onward, 2, groups)

    shares = lax.all_to_all(items, ("x", "y"), split_axis=0, concat_axis=0, tiled=True)
    own_sum, other_sum = pl.pallas_call(
        sum_kernel,
        out_shape=(vmem((own_neg, width), F32), vmem((own_neg, width), F32)),
        in_specs=[whole()],
        out_specs=(whole(), whole()),
        compiler_params=params(),
        name="sum_shares",
    )(held(shares))
    other_sum = after(other_sum, recv2)
    recv_sum = lax.ppermute(other_sum, "zl", [(i, near - 1 - i) for i in range(near)])
    grad_items = pl.pallas_call(
        add_kernel,
        out_shape=jax.ShapeDtypeStruct((own_neg, width), F32),
        in_specs=[whole(), whole()],
        out_specs=whole(),
        compiler_params=params(),
        name="add_neighbour",
    )(held(own_sum), held(recv_sum))

    grad_query = pl.pallas_call(
        unpack_kernel,
        out_shape=jax.ShapeDtypeStruct((slots, LANES), BF16),
        in_specs=[small()] + [whole()] * 4,
        out_specs=anywhere(),
        scratch_shapes=[
            vmem((live + MAXLEN, LANES), F32),
            vmem((slots, LANES), BF16),
            pltpu.SemaphoreType.DMA((PARTS,)),
        ],
        compiler_params=params(),
        name="unpack",
    )(lengths, held(own), held(recv2), held(term), held(pt))
    return grad_query, grad_items


def solution(mesh, live=2048):
    split = Mesh(mesh.devices.reshape(4, 2, 4, mesh.shape["grp"]), SEQ + ("grp",))
    return jax.shard_map(
        partial(shards, live),
        mesh=split,
        in_specs=(
            P(SEQ, "grp"),
            P(SEQ, "grp"),
            P(SEQ),
            P(SEQ, None),
            P(SEQ + ("grp",), None),
            P(SEQ + ("grp",)),
        ),
        out_specs=(P(SEQ, "grp"), P(SEQ + ("grp",), None)),
        check_vma=False,
    )
```

```python
from functools import partial

import jax
import jax.numpy as jnp
from jax import lax
from jax.experimental import pallas as pl
from jax.experimental.pallas import tpu as pltpu
from jax.sharding import Mesh
from jax.sharding import PartitionSpec as P

MAXLEN = 192
LANES = 128
CHUNK = 64
TILE = 512
PARTS = 4
FLOOR = -1e30
MASKED = -3e38
SEQ = ("x", "zl", "y")
F32 = jnp.float32
BF16 = jnp.bfloat16
VMEM_BYTES = 14 * 1024 * 1024


def params():
    return pltpu.CompilerParams(vmem_limit_bytes=VMEM_BYTES)


def whole():
    return pl.BlockSpec(memory_space=pltpu.VMEM)


def anywhere():
    return pl.BlockSpec(memory_space=pl.ANY)


def small():
    return pl.BlockSpec(memory_space=pltpu.SMEM)


def dot(a, b, da, db):
    return lax.dot_general(a, b, (((da,), (db,)), ((), ())), preferred_element_type=F32)


def copy_rows(len_ref, src_ref, packed, first, last, start):
    for h in range(first, last):
        size = len_ref[0, h]
        for c in range(0, MAXLEN, CHUNK):

            @pl.when(size > c)
            def _():
                packed[pl.ds(start + c, CHUNK), :] = src_ref[h * MAXLEN + c : h * MAXLEN + c + CHUNK, :].astype(F32)

        start = start + size
    return start


def pass_on(value_ref, after_ref, out_ref):
    pass


def copies_kernel(row_ref, other_ref, out_ref):
    first = lax.axis_index("zl") == 0
    size = row_ref.shape[0]
    row, other = row_ref[...], other_ref[...]
    pair = (jnp.where(first, row, other), jnp.where(first, other, row))
    for i in range(out_ref.shape[0] // size):
        out_ref[i * size : (i + 1) * size, :] = pair[i % 2]


def sum_kernel(share_ref, own_ref, other_ref):
    first = lax.axis_index("zl") == 0
    size = own_ref.shape[0]
    totals = []
    for k in range(2):
        parts = [
            share_ref[i + k * size : i + (k + 1) * size, :].astype(F32)
            for i in range(0, share_ref.shape[0], 2 * size)
        ]
        while len(parts) > 1:
            parts = [a + b for a, b in zip(parts[::2], parts[1::2])]
        totals.append(parts[0])
    own_ref[...] = jnp.where(first, totals[0], totals[1])
    other_ref[...] = jnp.where(first, totals[1], totals[0])


def add_kernel(own_ref, recv_ref, out_ref):
    out_ref[...] = own_ref[...] + recv_ref[...]


def row_kernel(neg_ref, id_ref, out_ref, held_id, sems):
    rows, width = neg_ref.shape
    load_id = pltpu.make_async_copy(id_ref, held_id, sems.at[0])
    load = pltpu.make_async_copy(neg_ref, out_ref.at[:, pl.ds(0, width)], sems.at[1])
    load_id.start()
    load.start()
    load_id.wait()
    shape = (rows, LANES)
    lane = lax.broadcasted_iota(jnp.int32, shape, 1)
    ids = jnp.concatenate([held_id[...], jnp.zeros((1, LANES - rows), jnp.int32)], axis=1)
    own = lane == lax.broadcasted_iota(jnp.int32, shape, 0)
    value = jnp.sum(jnp.where(own, jnp.broadcast_to(ids, shape), 0), axis=1, keepdims=True)
    value = jnp.broadcast_to(value, shape)
    digit = jnp.where(lane == 0, value >> 16, jnp.where(lane == 1, (value >> 8) & 255, value & 255))
    out_ref[:, width:] = jnp.where(lane < 3, digit, 0).astype(F32).astype(BF16)
    load.wait()


def pack_query(len_ref, q_ref, qp_ref, held_q, held_len, packed, sems):
    parts = sems.shape[0] - 1
    size = q_ref.shape[0] // parts
    rows = [slice(i * size, (i + 1) * size) for i in range(parts)]
    loads = [pltpu.make_async_copy(q_ref.at[at], held_q.at[at], sems.at[i]) for i, at in enumerate(rows)]
    lengths = pltpu.make_async_copy(len_ref, held_len, sems.at[parts])
    lengths.start()
    for load in loads:
        load.start()
    lengths.wait()
    start = jnp.int32(0)
    per = size // MAXLEN
    for i, load in enumerate(loads):
        load.wait()
        start = copy_rows(held_len, held_q, packed, i * per, (i + 1) * per, start)
    qp_ref[...] = packed[: qp_ref.shape[0], :].astype(BF16)


def pack_positive(len_ref, p_ref, id_ref, qp_ref, pt_ref, part_ref, idp_ref, packed, ids):
    rows = qp_ref.shape[0]
    copy_rows(len_ref, p_ref, packed, 0, len_ref.shape[1], jnp.int32(0))
    ones = jnp.ones((16, LANES), BF16)
    for k in range(rows // LANES):
        at = slice(k * LANES, (k + 1) * LANES)
        held = packed[at, :]
        pt_ref[:, at] = held.T.astype(BF16)
        product = held * qp_ref[at, :].astype(F32)
        high = product.astype(BF16)
        low = (product - high.astype(F32)).astype(BF16)
        part_ref[:, at] = (dot(ones, high, 1, 1) + dot(ones, low, 1, 1))[:1, :]
    lane = lax.broadcasted_iota(jnp.int32, (1, LANES), 1)
    start = jnp.int32(0)
    for h in range(len_ref.shape[1]):
        row, off = divmod(h * MAXLEN, LANES)
        at = start + (LANES - off)
        target = at // LANES
        shift = at - target * LANES
        first = pltpu.roll(id_ref[row : row + 1, :], shift, 1)
        second = pltpu.roll(id_ref[row + 1 : row + 2, :], shift, 1)
        kept0 = ids[pl.ds(target, 1), :]
        kept1 = ids[pl.ds(target + 1, 1), :]
        ids[pl.ds(target, 1), :] = jnp.where(lane >= shift + off, first, kept0)
        ids[pl.ds(target + 1, 1), :] = jnp.where(
            lane + LANES >= shift + off, jnp.where(lane >= shift, second, first), kept1
        )
        ids[pl.ds(target + 2, 1), :] = second
        start = start + len_ref[0, h]
    for k in range(rows // LANES):
        idp_ref[:, k * LANES : (k + 1) * LANES] = ids[k + 1 : k + 2, :].astype(F32)


def block_of(order, step):
    return pl.ds(pl.multiple_of((order ^ step) * LANES, LANES), LANES)


def place_kernel(steps, *refs):
    member = lax.axis_index("grp")
    for step, ref in zip(steps, refs[:2]):
        refs[-1][:, block_of(member, step)] = ref[...]


def scores_kernel(neg_ref, qfull_ref, idp_ref, part_ref, e_ref, stat_ref, negid):
    width = 4 * LANES
    lane = lax.broadcasted_iota(jnp.int32, (1, LANES), 1)
    place = jnp.where(lane == 0, 65536.0, jnp.where(lane == 1, 256.0, jnp.where(lane == 2, 1.0, 0.0)))
    value = jnp.sum(neg_ref[:, width : width + LANES].astype(F32) * place, axis=1, keepdims=True)
    negid[...] = jnp.broadcast_to(value, negid.shape)
    e_ref[...] = dot(neg_ref[:, :width], qfull_ref[...], 1, 1)
    for k in range(e_ref.shape[1] // LANES):
        at = slice(k * LANES, (k + 1) * LANES)
        part = jnp.where(negid[...] == idp_ref[:, at], MASKED, e_ref[:, at])
        top = jnp.maximum(jnp.max(part, axis=0, keepdims=True), FLOOR)
        e = jnp.exp(part - top)
        e_ref[:, at] = e
        stat_ref[0:1, at] = top
        stat_ref[1:2, at] = jnp.sum(e, axis=0, keepdims=True)
    stat_ref[2:3, :] = part_ref[...]
    stat_ref[3:4, :] = part_ref[...]


def rows_kernel(neg_ref, e_ref, keep_ref, send_ref, turned):
    member = lax.axis_index("grp")
    half = 2 * LANES
    for k, step in enumerate((0, 2, 1, 3)):
        turned[k * LANES : (k + 1) * LANES, :] = neg_ref[:, block_of(member, step)].T
    for t in range(0, e_ref.shape[1], TILE):
        at = slice(t, t + TILE)
        out = dot(turned[...], e_ref[:, at].astype(BF16), 1, 0)
        keep_ref[:, at] = out[:half, :]
        send_ref[:, at] = out[half:, :].astype(BF16)


def merge_kernel(own_ref, other_ref, out_ref, own_scale, other_scale):
    top = jnp.maximum(own_ref[0:1, :], other_ref[0:1, :])
    mine, other = jnp.exp(own_ref[0:1, :] - top), jnp.exp(other_ref[0:1, :] - top)
    total = own_ref[1:2, :] * mine + other_ref[1:2, :] * other
    out_ref[0:1, :] = top
    out_ref[1:2, :] = total
    out_ref[2:3, :] = own_ref[2:3, :] + other_ref[2:3, :]
    out_ref[3:4, :] = total
    own_scale[...] = mine
    other_scale[...] = other


def norm_kernel(own, near, far, after_ref, own_scale, near_scale, far_scale, term_ref):
    positive = near[2:3, :] + far[2:3, :]
    top = jnp.maximum(jnp.maximum(near[0:1, :], far[0:1, :]), positive)
    total = jnp.exp(positive - top)
    for ref in (near, far):
        total = total + ref[1:2, :] * jnp.exp(ref[0:1, :] - top)
    log_total = top + jnp.log(total)
    own_scale[...] = jnp.exp(own[0:1, :] - log_total)
    near_scale[...] = jnp.exp(near[0:1, :] - log_total)
    far_scale[...] = jnp.exp(far[0:1, :] - log_total)
    term_ref[...] = jnp.exp(positive - log_total) - 1.0


def combine_kernel(scale_ref, other_ref, keep_ref, recv_ref, own_ref, send_ref):
    mine, other = scale_ref[...], other_ref[...]
    send_ref[...] = (keep_ref[LANES:, :] * mine + recv_ref[LANES:, :].astype(F32) * other).astype(BF16)
    own_ref[...] = keep_ref[:LANES, :] * mine + recv_ref[:LANES, :].astype(F32) * other


def items_kernel(scale_ref, e_ref, q_ref, out_ref):
    total = None
    for t in range(0, e_ref.shape[1], TILE):
        at = slice(t, t + TILE)
        weights = (e_ref[:, at] * scale_ref[:, at]).astype(BF16)
        part = dot(weights, q_ref[at, :], 1, 0)
        total = part if total is None else total + part
    out_ref[...] = total.astype(BF16)


def unpack_kernel(len_ref, own_ref, recv_ref, near, far, term_ref, pt_ref, out_ref, packed, staged, sems):
    rows = own_ref.shape[1]
    for k in range(rows // LANES):
        at = slice(k * LANES, (k + 1) * LANES)
        negatives = own_ref[:, at] * near[:, at] + recv_ref[:, at].astype(F32) * far[:, at]
        packed[at, :] = (negatives + term_ref[:, at] * pt_ref[:, at].astype(F32)).T
    index = lax.broadcasted_iota(jnp.int32, (CHUNK, LANES), 0)
    start = jnp.int32(0)
    parts = sems.shape[0]
    size = out_ref.shape[0] // parts
    stores = []
    for i in range(parts):
        for h in range(i * size // MAXLEN, (i + 1) * size // MAXLEN):
            count = len_ref[0, h]
            for c in range(0, MAXLEN, CHUNK):
                at = slice(h * MAXLEN + c, h * MAXLEN + c + CHUNK)

                @pl.when(count > c)
                def _():
                    live = jnp.where(index < count - c, packed[pl.ds(start + c, CHUNK), :], 0.0)
                    staged[at, :] = live.astype(BF16)

                @pl.when(count <= c)
                def _():
                    staged[at, :] = jnp.zeros((CHUNK, LANES), BF16)

            start = start + count
        at = slice(i * size, (i + 1) * size)
        stores.append(pltpu.make_async_copy(staged.at[at], out_ref.at[at], sems.at[i]))
        stores[-1].start()
    for store in stores:
        store.wait()


def held(value):
    return pltpu.with_memory_space_constraint(value, pltpu.VMEM)


def in_hbm(value):
    return pltpu.with_memory_space_constraint(value, pltpu.HBM)


def after(value, other):
    return pl.pallas_call(
        pass_on,
        out_shape=pltpu.VMEM(value.shape, value.dtype),
        in_specs=[anywhere()] * 2,
        out_specs=anywhere(),
        input_output_aliases={0: 0},
        compiler_params=params(),
        name="after",
    )(held(value), other)


def swap(value, step, groups):
    return lax.ppermute(value, "grp", [(g, g ^ step) for g in range(groups)])


def shards(live, query, pos_emb, pos_ids, lengths, negatives, neg_ids):
    groups = lax.axis_size("grp")
    seqs = lax.axis_size(SEQ)
    pair = lax.axis_size("zl")
    own_neg, width = negatives.shape
    slots = query.shape[0]
    negs = own_neg * seqs
    half = 2 * LANES
    vmem = pltpu.VMEM

    row = pl.pallas_call(
        row_kernel,
        out_shape=vmem((own_neg, width + LANES), BF16),
        in_specs=[anywhere()] * 2,
        out_specs=whole(),
        scratch_shapes=[vmem((1, own_neg), jnp.int32), pltpu.SemaphoreType.DMA((2,))],
        compiler_params=params(),
        name="negative_rows",
    )(in_hbm(negatives), in_hbm(neg_ids.reshape(1, own_neg)))

    other = lax.ppermute(row, "zl", [(i, pair - 1 - i) for i in range(pair)])
    qp = pl.pallas_call(
        pack_query,
        out_shape=vmem((live, LANES), BF16),
        in_specs=[anywhere()] * 2,
        out_specs=whole(),
        scratch_shapes=[
            vmem((slots, LANES), BF16),
            pltpu.SMEM(lengths.shape, jnp.int32),
            vmem((live + MAXLEN, LANES), F32),
            pltpu.SemaphoreType.DMA((PARTS + 1,)),
        ],
        compiler_params=params(),
        name="pack_query",
    )(in_hbm(lengths), in_hbm(query))
    qp = after(qp, other)
    q2 = swap(qp, 2, groups)
    pt, part, idp = pl.pallas_call(
        pack_positive,
        out_shape=(jax.ShapeDtypeStruct((LANES, live), BF16), vmem((1, live), F32), vmem((1, live), F32)),
        in_specs=[small(), whole(), whole(), whole()],
        out_specs=(whole(), whole(), whole()),
        scratch_shapes=[vmem((live + MAXLEN, LANES), F32), vmem((live // LANES + 8, LANES), jnp.int32)],
        compiler_params=params(),
        name="pack_positive",
    )(lengths, pos_emb, pos_ids.reshape(slots // LANES, LANES), held(qp))

    q2 = after(q2, part)
    qp = after(qp, q2)
    q1 = swap(qp, 1, groups)
    q3 = swap(q2, 1, groups)

    copies = pl.pallas_call(
        copies_kernel,
        out_shape=vmem((negs, width + LANES), BF16),
        in_specs=[whole()] * 2,
        out_specs=whole(),
        compiler_params=params(),
        name="copies",
    )(held(row), held(other))
    pool = lax.all_to_all(copies, ("x", "y"), split_axis=0, concat_axis=0, tiled=True)
    pool = held(pool)

    qfull = pl.pallas_call(
        partial(place_kernel, (0, 2)),
        out_shape=vmem((live, width), BF16),
        in_specs=[whole()] * 2,
        out_specs=whole(),
        compiler_params=params(),
        name="place_own",
    )(held(qp), held(q2))
    qfull = pl.pallas_call(
        partial(place_kernel, (1, 3)),
        out_shape=vmem((live, width), BF16),
        in_specs=[whole()] * 3,
        out_specs=whole(),
        input_output_aliases={2: 0},
        compiler_params=params(),
        name="place_near",
    )(held(q1), held(q3), held(qfull))
    qfull = held(qfull)
    e, stat = pl.pallas_call(
        scores_kernel,
        out_shape=(vmem((negs, live), F32), vmem((4, live), F32)),
        in_specs=[whole()] * 4,
        out_specs=(whole(), whole()),
        scratch_shapes=[vmem((negs, LANES), F32)],
        compiler_params=params(),
        name="scores",
    )(pool, qfull, held(idp), held(part))
    stat, stat1 = held(stat), held(swap(stat, 1, groups))
    near, own_part, other_part = pl.pallas_call(
        merge_kernel,
        out_shape=(vmem((4, live), F32), vmem((1, live), F32), vmem((1, live), F32)),
        in_specs=[whole()] * 2,
        out_specs=(whole(),) * 3,
        compiler_params=params(),
        name="merge_stats",
    )(stat, stat1)
    far = swap(near, 2, groups)

    keep, send = pl.pallas_call(
        rows_kernel,
        out_shape=(vmem((half, live), F32), vmem((half, live), BF16)),
        in_specs=[whole()] * 2,
        out_specs=(whole(), whole()),
        scratch_shapes=[vmem((width, negs), BF16)],
        compiler_params=params(),
        name="row_products",
    )(pool, held(e))
    recv = swap(after(send, stat1), 1, groups)
    own, onward = pl.pallas_call(
        combine_kernel,
        out_shape=(vmem((LANES, live), F32), vmem((LANES, live), BF16)),
        in_specs=[whole()] * 4,
        out_specs=(whole(), whole()),
        compiler_params=params(),
        name="combine",
    )(held(own_part), held(other_part), held(keep), held(recv))
    recv2 = swap(onward, 2, groups)

    own_scale, near_scale, far_scale, term = pl.pallas_call(
        norm_kernel,
        out_shape=(vmem((1, live), F32),) * 4,
        in_specs=[whole()] * 3 + [anywhere()],
        out_specs=(whole(),) * 4,
        compiler_params=params(),
        name="norm",
    )(stat, held(near), held(far), onward)
    items = pl.pallas_call(
        items_kernel,
        out_shape=vmem((negs, width), BF16),
        in_specs=[whole()] * 3,
        out_specs=whole(),
        compiler_params=params(),
        name="item_products",
    )(held(own_scale), held(e), qfull)
    shares = lax.all_to_all(items, ("x", "y"), split_axis=0, concat_axis=0, tiled=True)
    own_sum, other_sum = pl.pallas_call(
        sum_kernel,
        out_shape=(vmem((own_neg, width), F32), vmem((own_neg, width), F32)),
        in_specs=[whole()],
        out_specs=(whole(), whole()),
        compiler_params=params(),
        name="sum_shares",
    )(held(shares))
    other_sum = after(other_sum, recv2)
    recv_sum = lax.ppermute(other_sum, "zl", [(i, pair - 1 - i) for i in range(pair)])
    grad_items = pl.pallas_call(
        add_kernel,
        out_shape=jax.ShapeDtypeStruct((own_neg, width), F32),
        in_specs=[whole(), whole()],
        out_specs=whole(),
        compiler_params=params(),
        name="add_neighbour",
    )(held(own_sum), held(recv_sum))

    grad_query = pl.pallas_call(
        unpack_kernel,
        out_shape=jax.ShapeDtypeStruct((slots, LANES), BF16),
        in_specs=[small()] + [whole()] * 6,
        out_specs=anywhere(),
        scratch_shapes=[
            vmem((live + MAXLEN, LANES), F32),
            vmem((slots, LANES), BF16),
            pltpu.SemaphoreType.DMA((PARTS,)),
        ],
        compiler_params=params(),
        name="unpack",
    )(lengths, *[held(v) for v in (own, recv2, near_scale, far_scale, term, pt)])
    return grad_query, grad_items


def solution(mesh, live=2048):
    split = Mesh(mesh.devices.reshape(4, 2, 4, mesh.shape["grp"]), SEQ + ("grp",))
    return jax.shard_map(
        partial(shards, live),
        mesh=split,
        in_specs=(
            P(SEQ, "grp"),
            P(SEQ, "grp"),
            P(SEQ),
            P(SEQ, None),
            P(SEQ + ("grp",), None),
            P(SEQ + ("grp",)),
        ),
        out_specs=(P(SEQ, "grp"), P(SEQ + ("grp",), None)),
        check_vma=False,
    )
```

```python
from functools import partial

import jax
import jax.numpy as jnp
from jax import lax
from jax.experimental import pallas as pl
from jax.experimental.pallas import tpu as pltpu
from jax.sharding import Mesh
from jax.sharding import PartitionSpec as P

MAXLEN = 192
LANES = 128
CHUNK = 64
TILE = 512
SUB = 16
PARTS = 4
FLOOR = -1e30
MASKED = -3e38
SEQ = ("x", "zl", "y")
F32 = jnp.float32
BF16 = jnp.bfloat16
VMEM_BYTES = 14 * 1024 * 1024


def params():
    return pltpu.CompilerParams(vmem_limit_bytes=VMEM_BYTES)


def weight(micros):
    return pl.CostEstimate(flops=int(micros * 1e9), transcendentals=0, bytes_accessed=0)


def whole():
    return pl.BlockSpec(memory_space=pltpu.VMEM)


def anywhere():
    return pl.BlockSpec(memory_space=pl.ANY)


def small():
    return pl.BlockSpec(memory_space=pltpu.SMEM)


def dot(a, b, da, db):
    return lax.dot_general(a, b, (((da,), (db,)), ((), ())), preferred_element_type=F32)


def copy_rows(len_ref, src_ref, packed, first, last, start):
    for h in range(first, last):
        size = len_ref[0, h]
        for c in range(0, MAXLEN, CHUNK):

            @pl.when(size > c)
            def _():
                packed[pl.ds(start + c, CHUNK), :] = src_ref[h * MAXLEN + c : h * MAXLEN + c + CHUNK, :].astype(F32)

        start = start + size
    return start


def pass_on(value_ref, after_ref, out_ref):
    pass


def copies_kernel(row_ref, other_ref, out_ref):
    second = lax.axis_index("zl") == 1
    row, other = row_ref[...], other_ref[...]
    low, high = jnp.where(second, other, row), jnp.where(second, row, other)
    size = SUB
    parts = []
    for k in range(row_ref.shape[0] // size - 1):
        parts += [low[k * size : (k + 1) * size], high[k * size : (k + 1) * size]]
    parts.append((low[-size:].astype(F32) + pltpu.roll(high[-size:].astype(F32), 3, 1)).astype(BF16))
    for i in range(out_ref.shape[0] // size):
        out_ref[i * size : (i + 1) * size, :] = parts[i % len(parts)]


def sum_kernel(share_ref, own_ref, other_ref):
    first = lax.axis_index("zl") == 0
    size = own_ref.shape[0]
    totals = []
    for k in range(2):
        parts = [
            share_ref[i + k * size : i + (k + 1) * size, :].astype(F32)
            for i in range(0, share_ref.shape[0], 2 * size)
        ]
        while len(parts) > 1:
            parts = [a + b for a, b in zip(parts[::2], parts[1::2])]
        totals.append(parts[0])
    own_ref[...] = jnp.where(first, totals[0], totals[1])
    other_ref[...] = jnp.where(first, totals[1], totals[0])


def add_kernel(own_ref, recv_ref, out_ref):
    out_ref[...] = own_ref[...] + recv_ref[...]


def row_kernel(neg_ref, id_ref, out_ref, held_id, sems):
    rows, width = neg_ref.shape
    blocks = width // LANES
    loads = [pltpu.make_async_copy(id_ref, held_id, sems.at[blocks])]
    for k in range(blocks):
        src, dst = neg_ref.at[:, pl.ds(k * LANES, LANES)], out_ref.at[pl.ds(k * rows, rows)]
        loads.append(pltpu.make_async_copy(src, dst, sems.at[k]))
    for load in loads:
        load.start()
    loads[0].wait()
    shape = (rows, LANES)
    lane = lax.broadcasted_iota(jnp.int32, shape, 1)
    ids = jnp.concatenate([held_id[...], jnp.zeros((1, LANES - rows), jnp.int32)], axis=1)
    own = lane == lax.broadcasted_iota(jnp.int32, shape, 0)
    value = jnp.sum(jnp.where(own, jnp.broadcast_to(ids, shape), 0), axis=1, keepdims=True)
    value = jnp.broadcast_to(value, shape)
    digit = jnp.where(lane == 0, value >> 16, jnp.where(lane == 1, (value >> 8) & 255, value & 255))
    out_ref[blocks * rows :, :] = jnp.where(lane < 3, digit, 0).astype(F32).astype(BF16)
    for load in loads[1:]:
        load.wait()


def pack_query(len_ref, q_ref, qp_ref, held_q, held_len, packed, sems):
    parts = sems.shape[0] - 1
    size = q_ref.shape[0] // parts
    rows = [slice(i * size, (i + 1) * size) for i in range(parts)]
    loads = [pltpu.make_async_copy(q_ref.at[at], held_q.at[at], sems.at[i]) for i, at in enumerate(rows)]
    lengths = pltpu.make_async_copy(len_ref, held_len, sems.at[parts])
    lengths.start()
    for load in loads:
        load.start()
    lengths.wait()
    start = jnp.int32(0)
    per = size // MAXLEN
    for i, load in enumerate(loads):
        load.wait()
        start = copy_rows(held_len, held_q, packed, i * per, (i + 1) * per, start)
    qp_ref[...] = packed[: qp_ref.shape[0], :].astype(BF16)


def pack_positive(len_ref, p_ref, id_ref, qp_ref, pt_ref, part_ref, idp_ref, packed, ids):
    rows = qp_ref.shape[0]
    copy_rows(len_ref, p_ref, packed, 0, len_ref.shape[1], jnp.int32(0))
    ones = jnp.ones((16, LANES), BF16)
    for k in range(rows // LANES):
        at = slice(k * LANES, (k + 1) * LANES)
        held = packed[at, :]
        pt_ref[:, at] = held.T.astype(BF16)
        product = held * qp_ref[at, :].astype(F32)
        high = product.astype(BF16)
        low = (product - high.astype(F32)).astype(BF16)
        part_ref[:, at] = (dot(ones, high, 1, 1) + dot(ones, low, 1, 1))[:1, :]
    lane = lax.broadcasted_iota(jnp.int32, (1, LANES), 1)
    start = jnp.int32(0)
    for h in range(len_ref.shape[1]):
        row, off = divmod(h * MAXLEN, LANES)
        at = start + (LANES - off)
        target = at // LANES
        shift = at - target * LANES
        first = pltpu.roll(id_ref[row : row + 1, :], shift, 1)
        second = pltpu.roll(id_ref[row + 1 : row + 2, :], shift, 1)
        kept0 = ids[pl.ds(target, 1), :]
        kept1 = ids[pl.ds(target + 1, 1), :]
        ids[pl.ds(target, 1), :] = jnp.where(lane >= shift + off, first, kept0)
        ids[pl.ds(target + 1, 1), :] = jnp.where(
            lane + LANES >= shift + off, jnp.where(lane >= shift, second, first), kept1
        )
        ids[pl.ds(target + 2, 1), :] = second
        start = start + len_ref[0, h]
    for k in range(rows // LANES):
        idp_ref[:, k * LANES : (k + 1) * LANES] = ids[k + 1 : k + 2, :].astype(F32)


def block_of(order, step):
    return pl.ds(pl.multiple_of((order ^ step) * LANES, LANES), LANES)


def place_kernel(steps, *refs):
    member = lax.axis_index("grp")
    for step, ref in zip(steps, refs[:2]):
        refs[-1][:, block_of(member, step)] = ref[...]


def pool_kernel(msg_ref, neg_ref, negid, tiles):
    blocks, pair = neg_ref.shape[1] // LANES, 2 * SUB
    pairs = neg_ref.shape[0] // pair
    for p in range(pairs):
        base = p * (2 * blocks + 1) * SUB
        for k in range(blocks):
            block = msg_ref[base + k * pair : base + (k + 1) * pair, :]
            neg_ref[p * pair : (p + 1) * pair, k * LANES : (k + 1) * LANES] = block
        tiles[p * SUB : (p + 1) * SUB, :] = msg_ref[base + blocks * pair : base + blocks * pair + SUB, :]
    lane = lax.broadcasted_iota(jnp.int32, (2 * LANES, LANES), 1)
    place = lane - 3 * (lax.broadcasted_iota(jnp.int32, (2 * LANES, LANES), 0) // LANES)
    place = jnp.where(place == 0, 65536.0, jnp.where(place == 1, 256.0, jnp.where(place == 2, 1.0, 0.0)))
    value = dot(tiles[...], place.astype(BF16), 1, 1)
    for p in range(pairs):
        for k in range(2):
            at = p * pair + k * SUB
            negid[at : at + SUB, :] = value[p * SUB : (p + 1) * SUB, k * LANES : (k + 1) * LANES]


def scores_kernel(msg_ref, qfull_ref, idp_ref, part_ref, neg_ref, e_ref, stat_ref, negid, tiles):
    pool_kernel(msg_ref, neg_ref, negid, tiles)
    e_ref[...] = dot(neg_ref[...], qfull_ref[...], 1, 1)
    for k in range(e_ref.shape[1] // LANES):
        at = slice(k * LANES, (k + 1) * LANES)
        part = jnp.where(negid[...] == idp_ref[:, at], MASKED, e_ref[:, at])
        top = jnp.maximum(jnp.max(part, axis=0, keepdims=True), FLOOR)
        e = jnp.exp(part - top)
        e_ref[:, at] = e
        stat_ref[0:1, at] = top
        stat_ref[1:2, at] = jnp.sum(e, axis=0, keepdims=True)
    stat_ref[2:3, :] = part_ref[...]
    stat_ref[3:4, :] = part_ref[...]


def rows_kernel(neg_ref, e_ref, keep_ref, send_ref, turned):
    member = lax.axis_index("grp")
    half = 2 * LANES
    for k, step in enumerate((0, 2, 1, 3)):
        turned[k * LANES : (k + 1) * LANES, :] = neg_ref[:, block_of(member, step)].T
    for t in range(0, e_ref.shape[1], TILE):
        at = slice(t, t + TILE)
        out = dot(turned[...], e_ref[:, at].astype(BF16), 1, 0)
        keep_ref[:, at] = out[:half, :]
        send_ref[:, at] = out[half:, :].astype(BF16)


def merge_kernel(own_ref, other_ref, out_ref, own_scale, other_scale):
    top = jnp.maximum(own_ref[0:1, :], other_ref[0:1, :])
    mine, other = jnp.exp(own_ref[0:1, :] - top), jnp.exp(other_ref[0:1, :] - top)
    total = own_ref[1:2, :] * mine + other_ref[1:2, :] * other
    out_ref[0:1, :] = top
    out_ref[1:2, :] = total
    out_ref[2:3, :] = own_ref[2:3, :] + other_ref[2:3, :]
    out_ref[3:4, :] = total
    own_scale[...] = mine
    other_scale[...] = other


def norm_kernel(own, near, far, after_ref, own_scale, near_scale, far_scale, term_ref):
    positive = near[2:3, :] + far[2:3, :]
    top = jnp.maximum(jnp.maximum(near[0:1, :], far[0:1, :]), positive)
    total = jnp.exp(positive - top)
    for ref in (near, far):
        total = total + ref[1:2, :] * jnp.exp(ref[0:1, :] - top)
    log_total = top + jnp.log(total)
    own_scale[...] = jnp.exp(own[0:1, :] - log_total)
    near_scale[...] = jnp.exp(near[0:1, :] - log_total)
    far_scale[...] = jnp.exp(far[0:1, :] - log_total)
    term_ref[...] = jnp.exp(positive - log_total) - 1.0


def combine_kernel(scale_ref, other_ref, keep_ref, recv_ref, own_ref, send_ref):
    mine, other = scale_ref[...], other_ref[...]
    send_ref[...] = (keep_ref[LANES:, :] * mine + recv_ref[LANES:, :].astype(F32) * other).astype(BF16)
    own_ref[...] = keep_ref[:LANES, :] * mine + recv_ref[:LANES, :].astype(F32) * other


def items_kernel(scale_ref, e_ref, q_ref, out_ref):
    total = None
    for t in range(0, e_ref.shape[1], TILE):
        at = slice(t, t + TILE)
        weights = (e_ref[:, at] * scale_ref[:, at]).astype(BF16)
        part = dot(weights, q_ref[at, :], 1, 0)
        total = part if total is None else total + part
    out_ref[...] = total.astype(BF16)


def unpack_kernel(len_ref, own_ref, recv_ref, near, far, term_ref, pt_ref, out_ref, packed, staged, sems):
    rows = own_ref.shape[1]
    for k in range(rows // LANES):
        at = slice(k * LANES, (k + 1) * LANES)
        negatives = own_ref[:, at] * near[:, at] + recv_ref[:, at].astype(F32) * far[:, at]
        packed[at, :] = (negatives + term_ref[:, at] * pt_ref[:, at].astype(F32)).T
    index = lax.broadcasted_iota(jnp.int32, (CHUNK, LANES), 0)
    start = jnp.int32(0)
    parts = sems.shape[0]
    size = out_ref.shape[0] // parts
    stores = []
    for i in range(parts):
        for h in range(i * size // MAXLEN, (i + 1) * size // MAXLEN):
            count = len_ref[0, h]
            for c in range(0, MAXLEN, CHUNK):
                at = slice(h * MAXLEN + c, h * MAXLEN + c + CHUNK)

                @pl.when(count > c)
                def _():
                    live = jnp.where(index < count - c, packed[pl.ds(start + c, CHUNK), :], 0.0)
                    staged[at, :] = live.astype(BF16)

                @pl.when(count <= c)
                def _():
                    staged[at, :] = jnp.zeros((CHUNK, LANES), BF16)

            start = start + count
        at = slice(i * size, (i + 1) * size)
        stores.append(pltpu.make_async_copy(staged.at[at], out_ref.at[at], sems.at[i]))
        stores[-1].start()
    for store in stores:
        store.wait()


def held(value):
    return pltpu.with_memory_space_constraint(value, pltpu.VMEM)


def in_hbm(value):
    return pltpu.with_memory_space_constraint(value, pltpu.HBM)


def after(value, other):
    return pl.pallas_call(
        pass_on,
        out_shape=pltpu.VMEM(value.shape, value.dtype),
        in_specs=[anywhere()] * 2,
        out_specs=anywhere(),
        input_output_aliases={0: 0},
        compiler_params=params(),
        name="after",
    )(held(value), other)


def swap(value, step, groups):
    return lax.ppermute(value, "grp", [(g, g ^ step) for g in range(groups)])


def shards(live, query, pos_emb, pos_ids, lengths, negatives, neg_ids):
    groups = lax.axis_size("grp")
    seqs = lax.axis_size(SEQ)
    pair = lax.axis_size("zl")
    own_neg, width = negatives.shape
    slots = query.shape[0]
    negs = own_neg * seqs
    half, blocks = 2 * LANES, width // LANES
    vmem = pltpu.VMEM

    row = pl.pallas_call(
        row_kernel,
        out_shape=vmem((own_neg * (blocks + 1), LANES), BF16),
        in_specs=[anywhere()] * 2,
        out_specs=whole(),
        scratch_shapes=[vmem((1, own_neg), jnp.int32), pltpu.SemaphoreType.DMA((blocks + 1,))],
        compiler_params=params(),
        name="negative_rows",
    )(in_hbm(negatives), in_hbm(neg_ids.reshape(1, own_neg)))

    other = lax.ppermute(row, "zl", [(i, pair - 1 - i) for i in range(pair)])
    qp = pl.pallas_call(
        pack_query,
        out_shape=vmem((live, LANES), BF16),
        in_specs=[anywhere()] * 2,
        out_specs=whole(),
        scratch_shapes=[
            vmem((slots, LANES), BF16),
            pltpu.SMEM(lengths.shape, jnp.int32),
            vmem((live + MAXLEN, LANES), F32),
            pltpu.SemaphoreType.DMA((PARTS + 1,)),
        ],
        compiler_params=params(),
        name="pack_query",
    )(in_hbm(lengths), in_hbm(query))
    qp = after(qp, other)
    q2 = swap(qp, 2, groups)
    pt, part, idp = pl.pallas_call(
        pack_positive,
        out_shape=(jax.ShapeDtypeStruct((LANES, live), BF16), vmem((1, live), F32), vmem((1, live), F32)),
        in_specs=[small(), whole(), whole(), whole()],
        out_specs=(whole(), whole(), whole()),
        scratch_shapes=[vmem((live + MAXLEN, LANES), F32), vmem((live // LANES + 8, LANES), jnp.int32)],
        cost_estimate=weight(10),
        compiler_params=params(),
        name="pack_positive",
    )(lengths, pos_emb, pos_ids.reshape(slots // LANES, LANES), held(qp))

    qp = after(qp, q2)
    q1 = swap(qp, 1, groups)
    q3 = swap(q2, 1, groups)

    copies = pl.pallas_call(
        copies_kernel,
        out_shape=vmem((negs // 2 * (2 * blocks + 1), LANES), BF16),
        in_specs=[whole()] * 2,
        out_specs=whole(),
        compiler_params=params(),
        name="copies",
    )(held(row), held(other))
    pool = lax.all_to_all(copies, ("x", "y"), split_axis=0, concat_axis=0, tiled=True)
    pool = held(pool)

    qfull = pl.pallas_call(
        partial(place_kernel, (0, 2)),
        out_shape=vmem((live, width), BF16),
        in_specs=[whole()] * 2,
        out_specs=whole(),
        compiler_params=params(),
        name="place_own",
    )(held(qp), held(q2))
    qfull = pl.pallas_call(
        partial(place_kernel, (1, 3)),
        out_shape=vmem((live, width), BF16),
        in_specs=[whole()] * 3,
        out_specs=whole(),
        input_output_aliases={2: 0},
        compiler_params=params(),
        name="place_near",
    )(held(q1), held(q3), held(qfull))
    qfull = held(qfull)
    pool, e, stat = pl.pallas_call(
        scores_kernel,
        out_shape=(vmem((negs, width), BF16), vmem((negs, live), F32), vmem((4, live), F32)),
        in_specs=[whole()] * 4,
        out_specs=(whole(),) * 3,
        scratch_shapes=[vmem((negs, LANES), F32), vmem((negs // 2, LANES), BF16)],
        compiler_params=params(),
        name="scores",
    )(pool, qfull, held(idp), held(part))
    stat, stat1 = held(stat), held(swap(stat, 1, groups))
    near, own_part, other_part = pl.pallas_call(
        merge_kernel,
        out_shape=(vmem((4, live), F32), vmem((1, live), F32), vmem((1, live), F32)),
        in_specs=[whole()] * 2,
        out_specs=(whole(),) * 3,
        compiler_params=params(),
        name="merge_stats",
    )(stat, stat1)
    far = swap(near, 2, groups)

    keep, send = pl.pallas_call(
        rows_kernel,
        out_shape=(vmem((half, live), F32), vmem((half, live), BF16)),
        in_specs=[whole()] * 2,
        out_specs=(whole(), whole()),
        scratch_shapes=[vmem((width, negs), BF16)],
        compiler_params=params(),
        name="row_products",
    )(held(pool), held(e))
    recv = swap(after(send, stat1), 1, groups)
    own, onward = pl.pallas_call(
        combine_kernel,
        out_shape=(vmem((LANES, live), F32), vmem((LANES, live), BF16)),
        in_specs=[whole()] * 4,
        out_specs=(whole(), whole()),
        compiler_params=params(),
        name="combine",
    )(held(own_part), held(other_part), held(keep), held(recv))
    recv2 = swap(onward, 2, groups)

    own_scale, near_scale, far_scale, term = pl.pallas_call(
        norm_kernel,
        out_shape=(vmem((1, live), F32),) * 4,
        in_specs=[whole()] * 3 + [anywhere()],
        out_specs=(whole(),) * 4,
        compiler_params=params(),
        name="norm",
    )(stat, held(near), held(far), onward)
    items = pl.pallas_call(
        items_kernel,
        out_shape=vmem((negs, width), BF16),
        in_specs=[whole()] * 3,
        out_specs=whole(),
        compiler_params=params(),
        name="item_products",
    )(held(own_scale), held(e), qfull)
    shares = lax.all_to_all(items, ("x", "y"), split_axis=0, concat_axis=0, tiled=True)
    own_sum, other_sum = pl.pallas_call(
        sum_kernel,
        out_shape=(vmem((own_neg, width), F32), vmem((own_neg, width), F32)),
        in_specs=[whole()],
        out_specs=(whole(), whole()),
        compiler_params=params(),
        name="sum_shares",
    )(held(shares))
    other_sum = after(other_sum, recv2)
    recv_sum = lax.ppermute(other_sum, "zl", [(i, pair - 1 - i) for i in range(pair)])
    grad_items = pl.pallas_call(
        add_kernel,
        out_shape=jax.ShapeDtypeStruct((own_neg, width), F32),
        in_specs=[whole(), whole()],
        out_specs=whole(),
        compiler_params=params(),
        name="add_neighbour",
    )(held(own_sum), held(recv_sum))

    grad_query = pl.pallas_call(
        unpack_kernel,
        out_shape=jax.ShapeDtypeStruct((slots, LANES), BF16),
        in_specs=[small()] + [whole()] * 6,
        out_specs=anywhere(),
        scratch_shapes=[
            vmem((live + MAXLEN, LANES), F32),
            vmem((slots, LANES), BF16),
            pltpu.SemaphoreType.DMA((PARTS,)),
        ],
        compiler_params=params(),
        name="unpack",
    )(lengths, *[held(v) for v in (own, recv2, near_scale, far_scale, term, pt)])
    return grad_query, grad_items


def solution(mesh, live=2048):
    split = Mesh(mesh.devices.reshape(4, 2, 4, mesh.shape["grp"]), SEQ + ("grp",))
    return jax.shard_map(
        partial(shards, live),
        mesh=split,
        in_specs=(
            P(SEQ, "grp"),
            P(SEQ, "grp"),
            P(SEQ),
            P(SEQ, None),
            P(SEQ + ("grp",), None),
            P(SEQ + ("grp",)),
        ),
        out_specs=(P(SEQ, "grp"), P(SEQ + ("grp",), None)),
        check_vma=False,
    )
```

```python
from functools import partial

import jax
import jax.numpy as jnp
from jax import lax
from jax.experimental import pallas as pl
from jax.experimental.pallas import tpu as pltpu
from jax.sharding import Mesh
from jax.sharding import PartitionSpec as P

MAXLEN = 192
LANES = 128
CHUNK = 192
TILE = 512
SUB = 16
PARTS = 4
FLOOR = -1e30
MASKED = -3e38
SEQ = ("x", "zl", "y")
F32 = jnp.float32
BF16 = jnp.bfloat16
VMEM_BYTES = 14 * 1024 * 1024


def params():
    return pltpu.CompilerParams(vmem_limit_bytes=VMEM_BYTES)


def weight(micros):
    return pl.CostEstimate(flops=int(micros * 1e9), transcendentals=0, bytes_accessed=0)


def whole():
    return pl.BlockSpec(memory_space=pltpu.VMEM)


def anywhere():
    return pl.BlockSpec(memory_space=pl.ANY)


def small():
    return pl.BlockSpec(memory_space=pltpu.SMEM)


def dot(a, b, da, db):
    return lax.dot_general(a, b, (((da,), (db,)), ((), ())), preferred_element_type=F32)


def copy_rows(len_ref, src_ref, packed, first, last, start):
    for h in range(first, last):
        size = len_ref[0, h]
        for c in range(0, MAXLEN, CHUNK):

            @pl.when(size > c)
            def _():
                packed[pl.ds(start + c, CHUNK), :] = src_ref[h * MAXLEN + c : h * MAXLEN + c + CHUNK, :].astype(F32)

        start = start + size
    return start


def pass_on(value_ref, after_ref, out_ref):
    pass


def copies_kernel(row_ref, other_ref, out_ref):
    second = lax.axis_index("zl") == 1
    row, other = row_ref[...], other_ref[...]
    low, high = jnp.where(second, other, row), jnp.where(second, row, other)
    size = SUB
    parts = []
    for k in range(row_ref.shape[0] // size - 1):
        parts += [low[k * size : (k + 1) * size], high[k * size : (k + 1) * size]]
    parts.append((low[-size:].astype(F32) + pltpu.roll(high[-size:].astype(F32), 3, 1)).astype(BF16))
    for i in range(out_ref.shape[0] // size):
        out_ref[i * size : (i + 1) * size, :] = parts[i % len(parts)]


def sum_kernel(share_ref, own_ref, other_ref):
    first = lax.axis_index("zl") == 0
    size = own_ref.shape[0]
    totals = []
    for k in range(2):
        parts = [
            share_ref[i + k * size : i + (k + 1) * size, :].astype(F32)
            for i in range(0, share_ref.shape[0], 2 * size)
        ]
        while len(parts) > 1:
            parts = [a + b for a, b in zip(parts[::2], parts[1::2])]
        totals.append(parts[0])
    own_ref[...] = jnp.where(first, totals[0], totals[1])
    other_ref[...] = jnp.where(first, totals[1], totals[0])


def add_kernel(own_ref, recv_ref, out_ref):
    out_ref[...] = own_ref[...] + recv_ref[...]


def row_kernel(neg_ref, id_ref, out_ref, held_id, sems):
    rows, width = neg_ref.shape
    blocks = width // LANES
    loads = [pltpu.make_async_copy(id_ref, held_id, sems.at[blocks])]
    for k in range(blocks):
        src, dst = neg_ref.at[:, pl.ds(k * LANES, LANES)], out_ref.at[pl.ds(k * rows, rows)]
        loads.append(pltpu.make_async_copy(src, dst, sems.at[k]))
    for load in loads:
        load.start()
    loads[0].wait()
    shape = (rows, LANES)
    lane = lax.broadcasted_iota(jnp.int32, shape, 1)
    ids = jnp.concatenate([held_id[...], jnp.zeros((1, LANES - rows), jnp.int32)], axis=1)
    own = lane == lax.broadcasted_iota(jnp.int32, shape, 0)
    value = jnp.sum(jnp.where(own, jnp.broadcast_to(ids, shape), 0), axis=1, keepdims=True)
    value = jnp.broadcast_to(value, shape)
    digit = jnp.where(lane == 0, value >> 16, jnp.where(lane == 1, (value >> 8) & 255, value & 255))
    out_ref[blocks * rows :, :] = jnp.where(lane < 3, digit, 0).astype(F32).astype(BF16)
    for load in loads[1:]:
        load.wait()


def pack_query(len_ref, q_ref, qp_ref, held_q, held_len, packed, sems):
    parts = sems.shape[0] - 1
    size = q_ref.shape[0] // parts
    rows = [slice(i * size, (i + 1) * size) for i in range(parts)]
    loads = [pltpu.make_async_copy(q_ref.at[at], held_q.at[at], sems.at[i]) for i, at in enumerate(rows)]
    lengths = pltpu.make_async_copy(len_ref, held_len, sems.at[parts])
    lengths.start()
    for load in loads:
        load.start()
    lengths.wait()
    start = jnp.int32(0)
    per = size // MAXLEN
    for i, load in enumerate(loads):
        load.wait()
        start = copy_rows(held_len, held_q, packed, i * per, (i + 1) * per, start)
    qp_ref[...] = packed[: qp_ref.shape[0], :].astype(BF16)


def pack_positive(len_ref, p_ref, id_ref, qp_ref, pt_ref, part_ref, idp_ref, packed, ids):
    rows = qp_ref.shape[0]
    copy_rows(len_ref, p_ref, packed, 0, len_ref.shape[1], jnp.int32(0))
    ones = jnp.ones((16, LANES), BF16)
    for k in range(rows // LANES):
        at = slice(k * LANES, (k + 1) * LANES)
        held = packed[at, :]
        pt_ref[:, at] = held.T.astype(BF16)
        product = held * qp_ref[at, :].astype(F32)
        high = product.astype(BF16)
        low = (product - high.astype(F32)).astype(BF16)
        part_ref[:, at] = (dot(ones, high, 1, 1) + dot(ones, low, 1, 1))[:1, :]
    lane = lax.broadcasted_iota(jnp.int32, (1, LANES), 1)
    start = jnp.int32(0)
    for h in range(len_ref.shape[1]):
        row, off = divmod(h * MAXLEN, LANES)
        at = start + (LANES - off)
        target = at // LANES
        shift = at - target * LANES
        first = pltpu.roll(id_ref[row : row + 1, :], shift, 1)
        second = pltpu.roll(id_ref[row + 1 : row + 2, :], shift, 1)
        kept0 = ids[pl.ds(target, 1), :]
        kept1 = ids[pl.ds(target + 1, 1), :]
        ids[pl.ds(target, 1), :] = jnp.where(lane >= shift + off, first, kept0)
        ids[pl.ds(target + 1, 1), :] = jnp.where(
            lane + LANES >= shift + off, jnp.where(lane >= shift, second, first), kept1
        )
        ids[pl.ds(target + 2, 1), :] = second
        start = start + len_ref[0, h]
    for k in range(rows // LANES):
        idp_ref[:, k * LANES : (k + 1) * LANES] = ids[k + 1 : k + 2, :].astype(F32)


def block_of(order, step):
    return pl.ds(pl.multiple_of((order ^ step) * LANES, LANES), LANES)


def place_kernel(steps, *refs):
    member = lax.axis_index("grp")
    for step, ref in zip(steps, refs[:2]):
        refs[-1][:, block_of(member, step)] = ref[...]


def pool_kernel(msg_ref, neg_ref, negid, tiles):
    blocks, pair = neg_ref.shape[1] // LANES, 2 * SUB
    pairs = neg_ref.shape[0] // pair
    for p in range(pairs):
        base = p * (2 * blocks + 1) * SUB
        for k in range(blocks):
            block = msg_ref[base + k * pair : base + (k + 1) * pair, :]
            neg_ref[p * pair : (p + 1) * pair, k * LANES : (k + 1) * LANES] = block
        tiles[p * SUB : (p + 1) * SUB, :] = msg_ref[base + blocks * pair : base + blocks * pair + SUB, :]
    lane = lax.broadcasted_iota(jnp.int32, (2 * LANES, LANES), 1)
    place = lane - 3 * (lax.broadcasted_iota(jnp.int32, (2 * LANES, LANES), 0) // LANES)
    place = jnp.where(place == 0, 65536.0, jnp.where(place == 1, 256.0, jnp.where(place == 2, 1.0, 0.0)))
    value = dot(tiles[...], place.astype(BF16), 1, 1)
    for p in range(pairs):
        for k in range(2):
            at = p * pair + k * SUB
            negid[at : at + SUB, :] = value[p * SUB : (p + 1) * SUB, k * LANES : (k + 1) * LANES]


def scores_kernel(msg_ref, qfull_ref, idp_ref, part_ref, neg_ref, e_ref, stat_ref, negid, tiles):
    pool_kernel(msg_ref, neg_ref, negid, tiles)
    e_ref[...] = dot(neg_ref[...], qfull_ref[...], 1, 1)
    for k in range(e_ref.shape[1] // LANES):
        at = slice(k * LANES, (k + 1) * LANES)
        part = jnp.where(negid[...] == idp_ref[:, at], MASKED, e_ref[:, at])
        top = jnp.maximum(jnp.max(part, axis=0, keepdims=True), FLOOR)
        e = jnp.exp(part - top)
        e_ref[:, at] = e
        stat_ref[0:1, at] = top
        stat_ref[1:2, at] = jnp.sum(e, axis=0, keepdims=True)
    stat_ref[2:3, :] = part_ref[...]
    stat_ref[3:4, :] = part_ref[...]


def rows_kernel(neg_ref, e_ref, keep_ref, send_ref, turned):
    member = lax.axis_index("grp")
    half = 2 * LANES
    for k, step in enumerate((0, 2, 1, 3)):
        turned[k * LANES : (k + 1) * LANES, :] = neg_ref[:, block_of(member, step)].T
    for t in range(0, e_ref.shape[1], TILE):
        at = slice(t, t + TILE)
        out = dot(turned[...], e_ref[:, at].astype(BF16), 1, 0)
        keep_ref[:, at] = out[:half, :]
        send_ref[:, at] = out[half:, :].astype(BF16)


def merge_kernel(own_ref, other_ref, out_ref, own_scale, other_scale):
    top = jnp.maximum(own_ref[0:1, :], other_ref[0:1, :])
    mine, other = jnp.exp(own_ref[0:1, :] - top), jnp.exp(other_ref[0:1, :] - top)
    total = own_ref[1:2, :] * mine + other_ref[1:2, :] * other
    out_ref[0:1, :] = top
    out_ref[1:2, :] = total
    out_ref[2:3, :] = own_ref[2:3, :] + other_ref[2:3, :]
    out_ref[3:4, :] = total
    own_scale[...] = mine
    other_scale[...] = other


def norm_kernel(own, near, far, after_ref, own_scale, near_scale, far_scale, term_ref):
    positive = near[2:3, :] + far[2:3, :]
    top = jnp.maximum(jnp.maximum(near[0:1, :], far[0:1, :]), positive)
    total = jnp.exp(positive - top)
    for ref in (near, far):
        total = total + ref[1:2, :] * jnp.exp(ref[0:1, :] - top)
    log_total = top + jnp.log(total)
    own_scale[...] = jnp.exp(own[0:1, :] - log_total)
    near_scale[...] = jnp.exp(near[0:1, :] - log_total)
    far_scale[...] = jnp.exp(far[0:1, :] - log_total)
    term_ref[...] = jnp.exp(positive - log_total) - 1.0


def combine_kernel(scale_ref, other_ref, keep_ref, recv_ref, own_ref, send_ref):
    mine, other = scale_ref[...], other_ref[...]
    send_ref[...] = (keep_ref[LANES:, :] * mine + recv_ref[LANES:, :].astype(F32) * other).astype(BF16)
    own_ref[...] = keep_ref[:LANES, :] * mine + recv_ref[:LANES, :].astype(F32) * other


def items_kernel(scale_ref, e_ref, q_ref, out_ref):
    total = None
    for t in range(0, e_ref.shape[1], TILE):
        at = slice(t, t + TILE)
        weights = (e_ref[:, at] * scale_ref[:, at]).astype(BF16)
        part = dot(weights, q_ref[at, :], 1, 0)
        total = part if total is None else total + part
    out_ref[...] = total.astype(BF16)


def unpack_kernel(len_ref, own_ref, recv_ref, near, far, term_ref, pt_ref, out_ref, packed, staged, sems):
    rows = own_ref.shape[1]
    for k in range(rows // LANES):
        at = slice(k * LANES, (k + 1) * LANES)
        negatives = own_ref[:, at] * near[:, at] + recv_ref[:, at].astype(F32) * far[:, at]
        packed[at, :] = (negatives + term_ref[:, at] * pt_ref[:, at].astype(F32)).T
    index = lax.broadcasted_iota(jnp.int32, (CHUNK, LANES), 0)
    start = jnp.int32(0)
    parts = sems.shape[0]
    size = out_ref.shape[0] // parts
    stores = []
    for i in range(parts):
        for h in range(i * size // MAXLEN, (i + 1) * size // MAXLEN):
            count = len_ref[0, h]
            for c in range(0, MAXLEN, CHUNK):
                at = slice(h * MAXLEN + c, h * MAXLEN + c + CHUNK)

                @pl.when(count > c)
                def _():
                    live = jnp.where(index < count - c, packed[pl.ds(start + c, CHUNK), :], 0.0)
                    staged[at, :] = live.astype(BF16)

                @pl.when(count <= c)
                def _():
                    staged[at, :] = jnp.zeros((CHUNK, LANES), BF16)

            start = start + count
        at = slice(i * size, (i + 1) * size)
        stores.append(pltpu.make_async_copy(staged.at[at], out_ref.at[at], sems.at[i]))
        stores[-1].start()
    for store in stores:
        store.wait()


def held(value):
    return pltpu.with_memory_space_constraint(value, pltpu.VMEM)


def in_hbm(value):
    return pltpu.with_memory_space_constraint(value, pltpu.HBM)


def after(value, other):
    return pl.pallas_call(
        pass_on,
        out_shape=pltpu.VMEM(value.shape, value.dtype),
        in_specs=[anywhere()] * 2,
        out_specs=anywhere(),
        input_output_aliases={0: 0},
        compiler_params=params(),
        name="after",
    )(held(value), other)


def swap(value, step, groups):
    return lax.ppermute(value, "grp", [(g, g ^ step) for g in range(groups)])


def shards(live, query, pos_emb, pos_ids, lengths, negatives, neg_ids):
    groups = lax.axis_size("grp")
    seqs = lax.axis_size(SEQ)
    pair = lax.axis_size("zl")
    own_neg, width = negatives.shape
    slots = query.shape[0]
    negs = own_neg * seqs
    half, blocks = 2 * LANES, width // LANES
    vmem = pltpu.VMEM

    row = pl.pallas_call(
        row_kernel,
        out_shape=vmem((own_neg * (blocks + 1), LANES), BF16),
        in_specs=[anywhere()] * 2,
        out_specs=whole(),
        scratch_shapes=[vmem((1, own_neg), jnp.int32), pltpu.SemaphoreType.DMA((blocks + 1,))],
        compiler_params=params(),
        name="negative_rows",
    )(in_hbm(negatives), in_hbm(neg_ids.reshape(1, own_neg)))

    other = lax.ppermute(row, "zl", [(i, pair - 1 - i) for i in range(pair)])
    qp = pl.pallas_call(
        pack_query,
        out_shape=vmem((live, LANES), BF16),
        in_specs=[anywhere()] * 2,
        out_specs=whole(),
        scratch_shapes=[
            vmem((slots, LANES), BF16),
            pltpu.SMEM(lengths.shape, jnp.int32),
            vmem((live + MAXLEN, LANES), F32),
            pltpu.SemaphoreType.DMA((PARTS + 1,)),
        ],
        compiler_params=params(),
        name="pack_query",
    )(in_hbm(lengths), in_hbm(query))
    qp = after(qp, other)
    q2 = swap(qp, 2, groups)
    pt, part, idp = pl.pallas_call(
        pack_positive,
        out_shape=(jax.ShapeDtypeStruct((LANES, live), BF16), vmem((1, live), F32), vmem((1, live), F32)),
        in_specs=[small(), whole(), whole(), whole()],
        out_specs=(whole(), whole(), whole()),
        scratch_shapes=[vmem((live + MAXLEN, LANES), F32), vmem((live // LANES + 8, LANES), jnp.int32)],
        cost_estimate=weight(10),
        compiler_params=params(),
        name="pack_positive",
    )(lengths, pos_emb, pos_ids.reshape(slots // LANES, LANES), held(qp))

    qp = after(qp, q2)
    q1 = swap(qp, 1, groups)
    q3 = swap(q2, 1, groups)

    copies = pl.pallas_call(
        copies_kernel,
        out_shape=vmem((negs // 2 * (2 * blocks + 1), LANES), BF16),
        in_specs=[whole()] * 2,
        out_specs=whole(),
        compiler_params=params(),
        name="copies",
    )(held(row), held(other))
    pool = lax.all_to_all(copies, ("x", "y"), split_axis=0, concat_axis=0, tiled=True)
    pool = held(pool)

    qfull = pl.pallas_call(
        partial(place_kernel, (0, 2)),
        out_shape=vmem((live, width), BF16),
        in_specs=[whole()] * 2,
        out_specs=whole(),
        compiler_params=params(),
        name="place_own",
    )(held(qp), held(q2))
    qfull = pl.pallas_call(
        partial(place_kernel, (1, 3)),
        out_shape=vmem((live, width), BF16),
        in_specs=[whole()] * 3,
        out_specs=whole(),
        input_output_aliases={2: 0},
        compiler_params=params(),
        name="place_near",
    )(held(q1), held(q3), held(qfull))
    qfull = held(qfull)
    pool, e, stat = pl.pallas_call(
        scores_kernel,
        out_shape=(vmem((negs, width), BF16), vmem((negs, live), F32), vmem((4, live), F32)),
        in_specs=[whole()] * 4,
        out_specs=(whole(),) * 3,
        scratch_shapes=[vmem((negs, LANES), F32), vmem((negs // 2, LANES), BF16)],
        compiler_params=params(),
        name="scores",
    )(pool, qfull, held(idp), held(part))
    stat, stat1 = held(stat), held(swap(stat, 1, groups))
    near, own_part, other_part = pl.pallas_call(
        merge_kernel,
        out_shape=(vmem((4, live), F32), vmem((1, live), F32), vmem((1, live), F32)),
        in_specs=[whole()] * 2,
        out_specs=(whole(),) * 3,
        compiler_params=params(),
        name="merge_stats",
    )(stat, stat1)
    far = swap(near, 2, groups)

    keep, send = pl.pallas_call(
        rows_kernel,
        out_shape=(vmem((half, live), F32), vmem((half, live), BF16)),
        in_specs=[whole()] * 2,
        out_specs=(whole(), whole()),
        scratch_shapes=[vmem((width, negs), BF16)],
        compiler_params=params(),
        name="row_products",
    )(held(pool), held(e))
    recv = swap(after(send, stat1), 1, groups)
    own, onward = pl.pallas_call(
        combine_kernel,
        out_shape=(vmem((LANES, live), F32), vmem((LANES, live), BF16)),
        in_specs=[whole()] * 4,
        out_specs=(whole(), whole()),
        compiler_params=params(),
        name="combine",
    )(held(own_part), held(other_part), held(keep), held(recv))
    recv2 = swap(onward, 2, groups)

    own_scale, near_scale, far_scale, term = pl.pallas_call(
        norm_kernel,
        out_shape=(vmem((1, live), F32),) * 4,
        in_specs=[whole()] * 3 + [anywhere()],
        out_specs=(whole(),) * 4,
        compiler_params=params(),
        name="norm",
    )(stat, held(near), held(far), onward)
    items = pl.pallas_call(
        items_kernel,
        out_shape=vmem((negs, width), BF16),
        in_specs=[whole()] * 3,
        out_specs=whole(),
        compiler_params=params(),
        name="item_products",
    )(held(own_scale), held(e), qfull)
    shares = lax.all_to_all(items, ("x", "y"), split_axis=0, concat_axis=0, tiled=True)
    own_sum, other_sum = pl.pallas_call(
        sum_kernel,
        out_shape=(vmem((own_neg, width), F32), vmem((own_neg, width), F32)),
        in_specs=[whole()],
        out_specs=(whole(), whole()),
        compiler_params=params(),
        name="sum_shares",
    )(held(shares))
    other_sum = after(other_sum, recv2)
    recv_sum = lax.ppermute(other_sum, "zl", [(i, pair - 1 - i) for i in range(pair)])
    grad_items = pl.pallas_call(
        add_kernel,
        out_shape=jax.ShapeDtypeStruct((own_neg, width), F32),
        in_specs=[whole(), whole()],
        out_specs=whole(),
        compiler_params=params(),
        name="add_neighbour",
    )(held(own_sum), held(recv_sum))

    grad_query = pl.pallas_call(
        unpack_kernel,
        out_shape=jax.ShapeDtypeStruct((slots, LANES), BF16),
        in_specs=[small()] + [whole()] * 6,
        out_specs=anywhere(),
        scratch_shapes=[
            vmem((live + MAXLEN, LANES), F32),
            vmem((slots, LANES), BF16),
            pltpu.SemaphoreType.DMA((PARTS,)),
        ],
        compiler_params=params(),
        name="unpack",
    )(lengths, *[held(v) for v in (own, recv2, near_scale, far_scale, term, pt)])
    return grad_query, grad_items


def solution(mesh, live=2048):
    split = Mesh(mesh.devices.reshape(4, 2, 4, mesh.shape["grp"]), SEQ + ("grp",))
    return jax.shard_map(
        partial(shards, live),
        mesh=split,
        in_specs=(
            P(SEQ, "grp"),
            P(SEQ, "grp"),
            P(SEQ),
            P(SEQ, None),
            P(SEQ + ("grp",), None),
            P(SEQ + ("grp",)),
        ),
        out_specs=(P(SEQ, "grp"), P(SEQ + ("grp",), None)),
        check_vma=False,
    )
```

```python
from functools import partial

import jax
import jax.numpy as jnp
from jax import lax
from jax.experimental import pallas as pl
from jax.experimental.pallas import tpu as pltpu
from jax.sharding import Mesh
from jax.sharding import PartitionSpec as P

MAXLEN = 192
LANES = 128
CHUNK = 192
TILE = 512
SUB = 16
PARTS = 4
FLOOR = -1e30
MASKED = -3e38
SEQ = ("x", "zl", "y")
F32 = jnp.float32
BF16 = jnp.bfloat16
VMEM_BYTES = 14 * 1024 * 1024


def params():
    return pltpu.CompilerParams(vmem_limit_bytes=VMEM_BYTES)


def weight(micros):
    return pl.CostEstimate(flops=int(micros * 1e9), transcendentals=0, bytes_accessed=0)


def whole():
    return pl.BlockSpec(memory_space=pltpu.VMEM)


def anywhere():
    return pl.BlockSpec(memory_space=pl.ANY)


def small():
    return pl.BlockSpec(memory_space=pltpu.SMEM)


def dot(a, b, da, db):
    return lax.dot_general(a, b, (((da,), (db,)), ((), ())), preferred_element_type=F32)


def copy_rows(len_ref, src_ref, packed, first, last, start):
    for h in range(first, last):
        size = len_ref[0, h]
        for c in range(0, MAXLEN, CHUNK):

            @pl.when(size > c)
            def _():
                packed[pl.ds(start + c, CHUNK), :] = src_ref[h * MAXLEN + c : h * MAXLEN + c + CHUNK, :].astype(F32)

        start = start + size
    return start


def pass_on(value_ref, after_ref, out_ref):
    pass


def copies_kernel(row_ref, other_ref, out_ref):
    second = lax.axis_index("zl") == 1
    row, other = row_ref[...], other_ref[...]
    low, high = jnp.where(second, other, row), jnp.where(second, row, other)
    size = SUB
    parts = []
    for k in range(row_ref.shape[0] // size - 1):
        parts += [low[k * size : (k + 1) * size], high[k * size : (k + 1) * size]]
    parts.append((low[-size:].astype(F32) + pltpu.roll(high[-size:].astype(F32), 3, 1)).astype(BF16))
    for i in range(out_ref.shape[0] // size):
        out_ref[i * size : (i + 1) * size, :] = parts[i % len(parts)]


def sum_kernel(share_ref, own_ref, other_ref):
    first = lax.axis_index("zl") == 0
    size = own_ref.shape[0]
    totals = []
    for k in range(2):
        parts = [
            share_ref[i + k * size : i + (k + 1) * size, :].astype(F32)
            for i in range(0, share_ref.shape[0], 2 * size)
        ]
        while len(parts) > 1:
            parts = [a + b for a, b in zip(parts[::2], parts[1::2])]
        totals.append(parts[0])
    own_ref[...] = jnp.where(first, totals[0], totals[1])
    other_ref[...] = jnp.where(first, totals[1], totals[0]).astype(BF16)


def add_kernel(own_ref, recv_ref, out_ref):
    out_ref[...] = own_ref[...] + recv_ref[...].astype(F32)


def row_kernel(neg_ref, id_ref, out_ref, held_id, sems):
    rows, width = neg_ref.shape
    blocks = width // LANES
    loads = [pltpu.make_async_copy(id_ref, held_id, sems.at[blocks])]
    for k in range(blocks):
        src, dst = neg_ref.at[:, pl.ds(k * LANES, LANES)], out_ref.at[pl.ds(k * rows, rows)]
        loads.append(pltpu.make_async_copy(src, dst, sems.at[k]))
    for load in loads:
        load.start()
    loads[0].wait()
    shape = (rows, LANES)
    lane = lax.broadcasted_iota(jnp.int32, shape, 1)
    ids = jnp.concatenate([held_id[...], jnp.zeros((1, LANES - rows), jnp.int32)], axis=1)
    own = lane == lax.broadcasted_iota(jnp.int32, shape, 0)
    value = jnp.sum(jnp.where(own, jnp.broadcast_to(ids, shape), 0), axis=1, keepdims=True)
    value = jnp.broadcast_to(value, shape)
    digit = jnp.where(lane == 0, value >> 16, jnp.where(lane == 1, (value >> 8) & 255, value & 255))
    out_ref[blocks * rows :, :] = jnp.where(lane < 3, digit, 0).astype(F32).astype(BF16)
    for load in loads[1:]:
        load.wait()


def pack_query(len_ref, q_ref, qp_ref, held_q, held_len, packed, sems):
    parts = sems.shape[0] - 1
    size = q_ref.shape[0] // parts
    rows = [slice(i * size, (i + 1) * size) for i in range(parts)]
    loads = [pltpu.make_async_copy(q_ref.at[at], held_q.at[at], sems.at[i]) for i, at in enumerate(rows)]
    lengths = pltpu.make_async_copy(len_ref, held_len, sems.at[parts])
    lengths.start()
    for load in loads:
        load.start()
    lengths.wait()
    start = jnp.int32(0)
    per = size // MAXLEN
    for i, load in enumerate(loads):
        load.wait()
        start = copy_rows(held_len, held_q, packed, i * per, (i + 1) * per, start)
    qp_ref[...] = packed[: qp_ref.shape[0], :].astype(BF16)


def pack_positive(len_ref, p_ref, id_ref, qp_ref, pt_ref, part_ref, idp_ref, packed, ids):
    rows = qp_ref.shape[0]
    copy_rows(len_ref, p_ref, packed, 0, len_ref.shape[1], jnp.int32(0))
    ones = jnp.ones((16, LANES), BF16)
    for k in range(rows // LANES):
        at = slice(k * LANES, (k + 1) * LANES)
        held = packed[at, :]
        pt_ref[:, at] = held.T.astype(BF16)
        product = held * qp_ref[at, :].astype(F32)
        high = product.astype(BF16)
        low = (product - high.astype(F32)).astype(BF16)
        part_ref[:, at] = (dot(ones, high, 1, 1) + dot(ones, low, 1, 1))[:1, :]
    lane = lax.broadcasted_iota(jnp.int32, (1, LANES), 1)
    start = jnp.int32(0)
    for h in range(len_ref.shape[1]):
        row, off = divmod(h * MAXLEN, LANES)
        at = start + (LANES - off)
        target = at // LANES
        shift = at - target * LANES
        first = pltpu.roll(id_ref[row : row + 1, :], shift, 1)
        second = pltpu.roll(id_ref[row + 1 : row + 2, :], shift, 1)
        kept0 = ids[pl.ds(target, 1), :]
        kept1 = ids[pl.ds(target + 1, 1), :]
        ids[pl.ds(target, 1), :] = jnp.where(lane >= shift + off, first, kept0)
        ids[pl.ds(target + 1, 1), :] = jnp.where(
            lane + LANES >= shift + off, jnp.where(lane >= shift, second, first), kept1
        )
        ids[pl.ds(target + 2, 1), :] = second
        start = start + len_ref[0, h]
    for k in range(rows // LANES):
        idp_ref[:, k * LANES : (k + 1) * LANES] = ids[k + 1 : k + 2, :].astype(F32)


def block_of(order, step):
    return pl.ds(pl.multiple_of((order ^ step) * LANES, LANES), LANES)


def place_kernel(steps, *refs):
    member = lax.axis_index("grp")
    for step, ref in zip(steps, refs[:2]):
        refs[-1][:, block_of(member, step)] = ref[...]


def pool_kernel(msg_ref, neg_ref, negid, tiles):
    blocks, pair = neg_ref.shape[1] // LANES, 2 * SUB
    pairs = neg_ref.shape[0] // pair
    for p in range(pairs):
        base = p * (2 * blocks + 1) * SUB
        for k in range(blocks):
            block = msg_ref[base + k * pair : base + (k + 1) * pair, :]
            neg_ref[p * pair : (p + 1) * pair, k * LANES : (k + 1) * LANES] = block
        tiles[p * SUB : (p + 1) * SUB, :] = msg_ref[base + blocks * pair : base + blocks * pair + SUB, :]
    lane = lax.broadcasted_iota(jnp.int32, (2 * LANES, LANES), 1)
    place = lane - 3 * (lax.broadcasted_iota(jnp.int32, (2 * LANES, LANES), 0) // LANES)
    place = jnp.where(place == 0, 65536.0, jnp.where(place == 1, 256.0, jnp.where(place == 2, 1.0, 0.0)))
    value = dot(tiles[...], place.astype(BF16), 1, 1)
    for p in range(pairs):
        for k in range(2):
            at = p * pair + k * SUB
            negid[at : at + SUB, :] = value[p * SUB : (p + 1) * SUB, k * LANES : (k + 1) * LANES]


def scores_kernel(msg_ref, qfull_ref, idp_ref, part_ref, neg_ref, e_ref, stat_ref, negid, tiles):
    pool_kernel(msg_ref, neg_ref, negid, tiles)
    e_ref[...] = dot(neg_ref[...], qfull_ref[...], 1, 1)
    for k in range(e_ref.shape[1] // LANES):
        at = slice(k * LANES, (k + 1) * LANES)
        part = jnp.where(negid[...] == idp_ref[:, at], MASKED, e_ref[:, at])
        top = jnp.maximum(jnp.max(part, axis=0, keepdims=True), FLOOR)
        e = jnp.exp(part - top)
        e_ref[:, at] = e
        stat_ref[0:1, at] = top
        stat_ref[1:2, at] = jnp.sum(e, axis=0, keepdims=True)
    stat_ref[2:3, :] = part_ref[...]
    stat_ref[3:4, :] = part_ref[...]


def rows_kernel(neg_ref, e_ref, keep_ref, send_ref, turned):
    member = lax.axis_index("grp")
    half = 2 * LANES
    for k, step in enumerate((0, 2, 1, 3)):
        turned[k * LANES : (k + 1) * LANES, :] = neg_ref[:, block_of(member, step)].T
    for t in range(0, e_ref.shape[1], TILE):
        at = slice(t, t + TILE)
        out = dot(turned[...], e_ref[:, at].astype(BF16), 1, 0)
        keep_ref[:, at] = out[:half, :]
        send_ref[:, at] = out[half:, :].astype(BF16)


def merge_kernel(own_ref, other_ref, out_ref, own_scale, other_scale):
    top = jnp.maximum(own_ref[0:1, :], other_ref[0:1, :])
    mine, other = jnp.exp(own_ref[0:1, :] - top), jnp.exp(other_ref[0:1, :] - top)
    total = own_ref[1:2, :] * mine + other_ref[1:2, :] * other
    out_ref[0:1, :] = top
    out_ref[1:2, :] = total
    out_ref[2:3, :] = own_ref[2:3, :] + other_ref[2:3, :]
    out_ref[3:4, :] = total
    own_scale[...] = mine
    other_scale[...] = other


def norm_kernel(own, near, far, after_ref, own_scale, near_scale, far_scale, term_ref):
    positive = near[2:3, :] + far[2:3, :]
    top = jnp.maximum(jnp.maximum(near[0:1, :], far[0:1, :]), positive)
    total = jnp.exp(positive - top)
    for ref in (near, far):
        total = total + ref[1:2, :] * jnp.exp(ref[0:1, :] - top)
    log_total = top + jnp.log(total)
    own_scale[...] = jnp.exp(own[0:1, :] - log_total)
    near_scale[...] = jnp.exp(near[0:1, :] - log_total)
    far_scale[...] = jnp.exp(far[0:1, :] - log_total)
    term_ref[...] = jnp.exp(positive - log_total) - 1.0


def combine_kernel(scale_ref, other_ref, keep_ref, recv_ref, own_ref, send_ref):
    mine, other = scale_ref[...], other_ref[...]
    send_ref[...] = (keep_ref[LANES:, :] * mine + recv_ref[LANES:, :].astype(F32) * other).astype(BF16)
    own_ref[...] = keep_ref[:LANES, :] * mine + recv_ref[:LANES, :].astype(F32) * other


def items_kernel(scale_ref, e_ref, q_ref, out_ref):
    total = None
    for t in range(0, e_ref.shape[1], TILE):
        at = slice(t, t + TILE)
        weights = (e_ref[:, at] * scale_ref[:, at]).astype(BF16)
        part = dot(weights, q_ref[at, :], 1, 0)
        total = part if total is None else total + part
    out_ref[...] = total.astype(BF16)


def unpack_kernel(len_ref, own_ref, recv_ref, near, far, term_ref, pt_ref, out_ref, packed, staged, sems):
    rows = own_ref.shape[1]
    for k in range(rows // LANES):
        at = slice(k * LANES, (k + 1) * LANES)
        negatives = own_ref[:, at] * near[:, at] + recv_ref[:, at].astype(F32) * far[:, at]
        packed[at, :] = (negatives + term_ref[:, at] * pt_ref[:, at].astype(F32)).T
    index = lax.broadcasted_iota(jnp.int32, (CHUNK, LANES), 0)
    start = jnp.int32(0)
    parts = sems.shape[0]
    size = out_ref.shape[0] // parts
    stores = []
    for i in range(parts):
        for h in range(i * size // MAXLEN, (i + 1) * size // MAXLEN):
            count = len_ref[0, h]
            for c in range(0, MAXLEN, CHUNK):
                at = slice(h * MAXLEN + c, h * MAXLEN + c + CHUNK)

                @pl.when(count > c)
                def _():
                    live = jnp.where(index < count - c, packed[pl.ds(start + c, CHUNK), :], 0.0)
                    staged[at, :] = live.astype(BF16)

                @pl.when(count <= c)
                def _():
                    staged[at, :] = jnp.zeros((CHUNK, LANES), BF16)

            start = start + count
        at = slice(i * size, (i + 1) * size)
        stores.append(pltpu.make_async_copy(staged.at[at], out_ref.at[at], sems.at[i]))
        stores[-1].start()
    for store in stores:
        store.wait()


def held(value):
    return pltpu.with_memory_space_constraint(value, pltpu.VMEM)


def in_hbm(value):
    return pltpu.with_memory_space_constraint(value, pltpu.HBM)


def after(value, other):
    return pl.pallas_call(
        pass_on,
        out_shape=pltpu.VMEM(value.shape, value.dtype),
        in_specs=[anywhere()] * 2,
        out_specs=anywhere(),
        input_output_aliases={0: 0},
        compiler_params=params(),
        name="after",
    )(held(value), other)


def swap(value, step, groups):
    return lax.ppermute(value, "grp", [(g, g ^ step) for g in range(groups)])


def shards(live, query, pos_emb, pos_ids, lengths, negatives, neg_ids):
    groups = lax.axis_size("grp")
    seqs = lax.axis_size(SEQ)
    pair = lax.axis_size("zl")
    own_neg, width = negatives.shape
    slots = query.shape[0]
    negs = own_neg * seqs
    half, blocks = 2 * LANES, width // LANES
    vmem = pltpu.VMEM

    row = pl.pallas_call(
        row_kernel,
        out_shape=vmem((own_neg * (blocks + 1), LANES), BF16),
        in_specs=[anywhere()] * 2,
        out_specs=whole(),
        scratch_shapes=[vmem((1, own_neg), jnp.int32), pltpu.SemaphoreType.DMA((blocks + 1,))],
        compiler_params=params(),
        name="negative_rows",
    )(in_hbm(negatives), in_hbm(neg_ids.reshape(1, own_neg)))

    other = lax.ppermute(row, "zl", [(i, pair - 1 - i) for i in range(pair)])
    qp = pl.pallas_call(
        pack_query,
        out_shape=vmem((live, LANES), BF16),
        in_specs=[anywhere()] * 2,
        out_specs=whole(),
        scratch_shapes=[
            vmem((slots, LANES), BF16),
            pltpu.SMEM(lengths.shape, jnp.int32),
            vmem((live + MAXLEN, LANES), F32),
            pltpu.SemaphoreType.DMA((PARTS + 1,)),
        ],
        compiler_params=params(),
        name="pack_query",
    )(in_hbm(lengths), in_hbm(query))
    qp = after(qp, other)
    q2 = swap(qp, 2, groups)
    pt, part, idp = pl.pallas_call(
        pack_positive,
        out_shape=(jax.ShapeDtypeStruct((LANES, live), BF16), vmem((1, live), F32), vmem((1, live), F32)),
        in_specs=[small(), whole(), whole(), whole()],
        out_specs=(whole(), whole(), whole()),
        scratch_shapes=[vmem((live + MAXLEN, LANES), F32), vmem((live // LANES + 8, LANES), jnp.int32)],
        cost_estimate=weight(10),
        compiler_params=params(),
        name="pack_positive",
    )(lengths, pos_emb, pos_ids.reshape(slots // LANES, LANES), held(qp))

    qp = after(qp, q2)
    q1 = swap(qp, 1, groups)
    q3 = swap(q2, 1, groups)

    copies = pl.pallas_call(
        copies_kernel,
        out_shape=vmem((negs // 2 * (2 * blocks + 1), LANES), BF16),
        in_specs=[whole()] * 2,
        out_specs=whole(),
        compiler_params=params(),
        name="copies",
    )(held(row), held(other))
    pool = lax.all_to_all(copies, ("x", "y"), split_axis=0, concat_axis=0, tiled=True)
    pool = held(pool)

    qfull = pl.pallas_call(
        partial(place_kernel, (0, 2)),
        out_shape=vmem((live, width), BF16),
        in_specs=[whole()] * 2,
        out_specs=whole(),
        compiler_params=params(),
        name="place_own",
    )(held(qp), held(q2))
    qfull = pl.pallas_call(
        partial(place_kernel, (1, 3)),
        out_shape=vmem((live, width), BF16),
        in_specs=[whole()] * 3,
        out_specs=whole(),
        input_output_aliases={2: 0},
        compiler_params=params(),
        name="place_near",
    )(held(q1), held(q3), held(qfull))
    qfull = held(qfull)
    pool, e, stat = pl.pallas_call(
        scores_kernel,
        out_shape=(vmem((negs, width), BF16), vmem((negs, live), F32), vmem((4, live), F32)),
        in_specs=[whole()] * 4,
        out_specs=(whole(),) * 3,
        scratch_shapes=[vmem((negs, LANES), F32), vmem((negs // 2, LANES), BF16)],
        compiler_params=params(),
        name="scores",
    )(pool, qfull, held(idp), held(part))
    stat, stat1 = held(stat), held(swap(stat, 1, groups))
    near, own_part, other_part = pl.pallas_call(
        merge_kernel,
        out_shape=(vmem((4, live), F32), vmem((1, live), F32), vmem((1, live), F32)),
        in_specs=[whole()] * 2,
        out_specs=(whole(),) * 3,
        compiler_params=params(),
        name="merge_stats",
    )(stat, stat1)
    far = swap(near, 2, groups)

    keep, send = pl.pallas_call(
        rows_kernel,
        out_shape=(vmem((half, live), F32), vmem((half, live), BF16)),
        in_specs=[whole()] * 2,
        out_specs=(whole(), whole()),
        scratch_shapes=[vmem((width, negs), BF16)],
        compiler_params=params(),
        name="row_products",
    )(held(pool), held(e))
    recv = swap(after(send, stat1), 1, groups)
    own, onward = pl.pallas_call(
        combine_kernel,
        out_shape=(vmem((LANES, live), F32), vmem((LANES, live), BF16)),
        in_specs=[whole()] * 4,
        out_specs=(whole(), whole()),
        compiler_params=params(),
        name="combine",
    )(held(own_part), held(other_part), held(keep), held(recv))
    recv2 = swap(onward, 2, groups)

    own_scale, near_scale, far_scale, term = pl.pallas_call(
        norm_kernel,
        out_shape=(vmem((1, live), F32),) * 4,
        in_specs=[whole()] * 3 + [anywhere()],
        out_specs=(whole(),) * 4,
        compiler_params=params(),
        name="norm",
    )(stat, held(near), held(far), onward)
    items = pl.pallas_call(
        items_kernel,
        out_shape=vmem((negs, width), BF16),
        in_specs=[whole()] * 3,
        out_specs=whole(),
        compiler_params=params(),
        name="item_products",
    )(held(own_scale), held(e), qfull)
    shares = lax.all_to_all(items, ("x", "y"), split_axis=0, concat_axis=0, tiled=True)
    own_sum, other_sum = pl.pallas_call(
        sum_kernel,
        out_shape=(vmem((own_neg, width), F32), vmem((own_neg, width), BF16)),
        in_specs=[whole()],
        out_specs=(whole(), whole()),
        compiler_params=params(),
        name="sum_shares",
    )(held(shares))
    other_sum = after(other_sum, recv2)
    recv_sum = lax.ppermute(other_sum, "zl", [(i, pair - 1 - i) for i in range(pair)])
    grad_items = pl.pallas_call(
        add_kernel,
        out_shape=jax.ShapeDtypeStruct((own_neg, width), F32),
        in_specs=[whole(), whole()],
        out_specs=whole(),
        compiler_params=params(),
        name="add_neighbour",
    )(held(own_sum), held(recv_sum))

    grad_query = pl.pallas_call(
        unpack_kernel,
        out_shape=jax.ShapeDtypeStruct((slots, LANES), BF16),
        in_specs=[small()] + [whole()] * 6,
        out_specs=anywhere(),
        scratch_shapes=[
            vmem((live + MAXLEN, LANES), F32),
            vmem((slots, LANES), BF16),
            pltpu.SemaphoreType.DMA((PARTS,)),
        ],
        compiler_params=params(),
        name="unpack",
    )(lengths, *[held(v) for v in (own, recv2, near_scale, far_scale, term, pt)])
    return grad_query, grad_items


def solution(mesh, live=2048):
    split = Mesh(mesh.devices.reshape(4, 2, 4, mesh.shape["grp"]), SEQ + ("grp",))
    return jax.shard_map(
        partial(shards, live),
        mesh=split,
        in_specs=(
            P(SEQ, "grp"),
            P(SEQ, "grp"),
            P(SEQ),
            P(SEQ, None),
            P(SEQ + ("grp",), None),
            P(SEQ + ("grp",)),
        ),
        out_specs=(P(SEQ, "grp"), P(SEQ + ("grp",), None)),
        check_vma=False,
    )
```
